32 devices in a mesh: lon: 8 (over y, x, core), lev: 4 (over z).
Axes of the slice: x: 2, y: 2, z: 4, core: 2. Of those that a mesh axis runs over, the one named last changes fastest.
Arguments:
- thickness: float32 [4, 128, 2048], P('lev', 'lon'), may hold values from 0.5 to 1.5
- wind_field: float32 [2, 4, 128, 2048], P(None, 'lev', 'lon'), may hold values from -3 to 3
Outputs:
- new_thickness: float32 [4, 128, 2048], P('lev', 'lon')
- new_winds: float32 [2, 4, 128, 2048], P(None, 'lev', 'lon')
The draws below stay inside these ranges and needn't reach their ends.
All inputs are finite; a program needn't handle non-finite values.
Results may differ from the reference program's by a relative error of at most 0.0001.
Values sent between devices are 32-bit elements; how exact they have to be, the bound alone decides.
No kernel may reach another device: no remote copies, remote signals or barrier semaphores. Data moves between devices by JAX's collectives and lax.ppermute only.
A program may use at most 64 MiB of HBM per device.

```python
import math
import jax
import jax.numpy as jnp
from jax import lax

NLAT = 2048
STEPS = 2
NLON = 128
LEV = 4
KMAX = 1365


def block_levels(key, shape, shards, smallest, high):
    gain = 1.0
    for dim, shards_of in shards:
        steps = jax.random.uniform(jax.random.fold_in(jax.random.fold_in(key, 6), dim), (shards_of,), jnp.float32, smallest / len(shards), high / len(shards))
        gain = gain * jnp.repeat(jnp.exp(steps), shape[dim] // shards_of).reshape((-1,) + (1,) * (len(shape) - 1 - dim))
    return gain


def gaussian(key, shape, deviation, limit, shards=(), held_as=jnp.bfloat16):
    level = block_levels(key, shape, shards, -0.22, 0.18) if shards else 1.0
    entries = jax.random.normal(key, shape, jnp.float32) * deviation * level
    return jnp.minimum(jnp.maximum(entries, -limit), limit).astype(held_as)


def setup_inputs(seed: int = 0) -> dict:
    key_of = jax.random.split(jax.random.key(seed), 3)
    thickness = jnp.clip(0.5 + 1.0 * jax.random.uniform(key_of[0], (LEV, NLON, NLAT), jnp.float32) ** block_levels(key_of[0], (LEV, NLON, NLAT), ((0, 4), (1, 8)), -0.2, 0.2), 0.5, 1.5)
    wind_field = gaussian(key_of[1], (2, LEV, NLON, NLAT), 0.5, 3.0, ((1, 4), (2, 8)), jnp.float32)
    return dict(thickness=thickness, wind_field=wind_field)


courant = 0.2
mixing = 0.25
coriolis = 0.5
cos_floor = 0.25
lon_weights = ((1, 45.0), (2, -9.0), (3, 1.0))


def lon_derivative(fields, axis_index):
    summed = jnp.zeros_like(fields)
    for offset, weight in lon_weights:
        summed = summed + weight * (jnp.roll(fields, -offset, axis_index) - jnp.roll(fields, offset, axis_index))
    return summed / 60.0


def spectral(fields):
    sign_column = jnp.array([1.0, -1.0, -1.0], dtype=fields.dtype).reshape(3, 1, 1)
    antipode = jnp.roll(fields, NLON // 2, 1)
    circle = jnp.concatenate([fields, sign_column * antipode[:, :, ::-1]], 2)
    length = 2 * NLAT
    spectrum = jnp.fft.rfft(circle, axis=2)
    wavenumbers = jnp.arange(NLAT + 1).astype(fields.dtype)
    retained = (wavenumbers <= KMAX).astype(fields.dtype)
    smooth = jnp.fft.irfft(spectrum * retained, n=length, axis=2)[:, :, :NLAT]
    factor = (2.0 * math.pi / length) * wavenumbers * retained
    meridional_slope = jnp.fft.irfft(spectrum * (1j * factor), n=length, axis=2)[:, :, :NLAT]
    return smooth.astype(fields.dtype), meridional_slope.astype(fields.dtype)


def level_update(fields, vertical, secant, coriolis_term):
    smooth, meridional_slope = spectral(fields)
    zonal_slope = lon_derivative(fields, 1)
    thickness_now = fields[0]
    eastward = fields[1]
    northward = fields[2]
    advect = eastward * secant * zonal_slope + northward * meridional_slope
    height_tendency = -advect[0] - thickness_now * (secant * zonal_slope[1] + meridional_slope[2]) + mixing * vertical
    east_tendency = -advect[1] - secant * zonal_slope[0] + coriolis_term * northward
    north_tendency = -advect[2] - meridional_slope[0] - coriolis_term * eastward
    return smooth + courant * jnp.stack([height_tendency, east_tendency, north_tendency])


def reference(thickness, wind_field):
    latitude = (jnp.arange(NLAT).astype(jnp.float32) + 0.5) * (math.pi / NLAT) - 0.5 * math.pi
    secant = 1.0 / jnp.maximum(jnp.cos(latitude), cos_floor)
    coriolis_term = coriolis * jnp.sin(latitude)
    fields_now = jnp.concatenate([thickness[None], wind_field], 0)
    for step_index in range(STEPS):
        padded = jnp.pad(fields_now[0], ((1, 1), (0, 0), (0, 0)))
        vertical = padded[2:] + padded[:-2] - 2.0 * fields_now[0]
        updated = lax.map(lambda level_pair: level_update(level_pair[0], level_pair[1], secant, coriolis_term), (jnp.swapaxes(fields_now, 0, 1), vertical))
        fields_now = jnp.swapaxes(updated, 0, 1)
    return fields_now[0], fields_now[1:]
```

```python
import functools
import math

import jax
import jax.numpy as jnp
import numpy as np
from jax import lax
from jax.experimental import pallas as pl
from jax.experimental.pallas import tpu as pltpu
from jax.sharding import PartitionSpec as P

STEPS = 2

courant = 0.2
mixing = 0.25
coriolis = 0.5
cos_floor = 0.25

RADIX = 128
ROWS = 8
HALO = 3
SIGNS = (1.0, -1.0, -1.0)


def split_table(table):
    high = table.astype(np.float32).astype(jnp.bfloat16)
    low = (table - high.astype(np.float64)).astype(np.float32).astype(jnp.bfloat16)
    return jnp.asarray(high), jnp.asarray(low)


@functools.lru_cache(maxsize=None)
def numpy_tables(lat_count):
    length = 2 * lat_count
    blocks = length // RADIX
    kept = blocks // 2 + 1
    centred = np.arange(RADIX) + 0.5
    order = np.arange(RADIX)
    signed = np.where(order < RADIX // 2, order, order - RADIX).astype(np.float64)
    angle = 2.0 * np.pi / RADIX * centred[:, None] * signed[None, :]
    cos, sin = np.cos(angle), np.sin(angle)
    forward = np.block([[cos, -sin], [sin, cos]])
    cos_t, sin_t = cos.T, sin.T
    weight = signed[:, None]
    inverse = np.block(
        [
            [cos_t, sin_t, -weight * sin_t, weight * cos_t],
            [-sin_t, cos_t, -weight * cos_t, -weight * sin_t],
        ]
    )
    first = np.arange(kept)
    turn = 2.0 * np.pi / length * first[:, None] * centred[None, :]
    twist = np.stack([np.cos(turn), -np.sin(turn)], 1)
    share = np.where((first == 0) | (first == blocks // 2), 1.0, 2.0)[:, None] / length
    back = np.stack([np.cos(turn) * share, np.sin(turn) * share], 1)
    slope_scale = 2.0 * np.pi * blocks / length
    back = np.concatenate([back, back * slope_scale], 1)
    wave = first[:, None] + blocks * signed[None, :]
    retained = (np.abs(wave) <= length // 3).astype(np.float64)
    plus = np.concatenate([retained, retained], 1)
    minus = np.concatenate([retained, -retained], 1)
    masks = np.stack([plus, minus, -minus], 1)
    latitude = (np.arange(lat_count) + 0.5) * (np.pi / lat_count) - 0.5 * np.pi
    rows = np.stack(
        [1.0 / np.maximum(np.cos(latitude), cos_floor), coriolis * np.sin(latitude)]
    )
    flat = lambda a: a.reshape(-1, a.shape[-1]).astype(np.float32)
    return forward, inverse, flat(twist), flat(back), flat(masks), rows.astype(np.float32)


def times(value, angle):
    real, imag = value
    cos, sin = math.cos(angle), math.sin(angle)
    quarter = round(angle / (math.pi / 2), 9)
    if quarter == int(quarter):
        turn = int(quarter) % 4
        return [(real, imag), (-imag, real), (-real, -imag), (imag, -real)][turn]
    if abs(abs(cos) - abs(sin)) < 1e-12:
        scale = abs(cos)
        a = real if cos > 0 else -real
        b = imag if cos > 0 else -imag
        c = imag if sin > 0 else -imag
        d = real if sin > 0 else -real
        return (scale * (a - c), scale * (b + d))
    return (real * cos - imag * sin, imag * cos + real * sin)


def add(a, b):
    return (a[0] + b[0], a[1] + b[1])


def sub(a, b):
    return (a[0] - b[0], a[1] - b[1])


def complex_dft(values, sign):
    n = len(values)
    if n == 1:
        return values
    half = n // 2
    even = complex_dft([add(values[m], values[m + half]) for m in range(half)], sign)
    odd = complex_dft(
        [
            times(sub(values[m], values[m + half]), sign * 2 * math.pi * m / n)
            for m in range(half)
        ],
        sign,
    )
    return [even[q // 2] if q % 2 == 0 else odd[q // 2] for q in range(n)]


def odd_outputs(values):
    r = len(values)
    if r == 1:
        return {1: (values[0], None)}
    half = r // 2
    turned = [
        times((values[m], -values[m + half]), -math.pi * m / r) for m in range(half)
    ]
    out = {}
    for q, value in enumerate(complex_dft(turned, -1)):
        j = 4 * q + 1
        out[j if j <= r else 2 * r - j] = value if j <= r else (value[0], -value[1])
    return out


def half_circle_forward(values):
    n = len(values)
    out = {j: value for j, value in odd_outputs(values).items()}
    scale = 2
    while len(values) > 1:
        half = len(values) // 2
        difference = [values[m] - values[m + half] for m in range(half)]
        values = [values[m] + values[m + half] for m in range(half)]
        for j, value in odd_outputs(difference).items():
            out[j * scale] = value
        scale *= 2
    out[0] = (values[0], None)
    return [out[k] for k in range(n + 1)]


def odd_inputs(values, r):
    if r == 1:
        return [values[1][0]]
    half = r // 2
    gathered = []
    for q in range(half):
        j = 4 * q + 1
        if j <= r:
            gathered.append(values[j])
        else:
            real, imag = values[2 * r - j]
            gathered.append((real, -imag))
    turned = [
        times(value, math.pi * m / r) for m, value in enumerate(complex_dft(gathered, 1))
    ]
    return [value[0] for value in turned] + [-value[1] for value in turned]


def half_circle_inverse(values):
    n = len(values) - 1
    result = [values[0][0]]
    size = 1
    while size < n:
        step = n // size
        difference = odd_inputs({j: values[j * step] for j in range(1, size + 1, 2)}, size)
        result = [result[m] + difference[m] for m in range(size)] + [
            result[m] - difference[m] for m in range(size)
        ]
        size *= 2
    last = odd_inputs({j: values[j] for j in range(1, n + 1, 2)}, n)
    return [result[m] + last[m] for m in range(n)]


def tile(index):
    return pl.ds(index * RADIX, RADIX)


def split(value):
    high = value.astype(jnp.bfloat16)
    return high, (value - high.astype(jnp.float32)).astype(jnp.bfloat16)


def triple_product(value, high_table, low_table):
    high, low = split(value)
    dot = functools.partial(jnp.dot, preferred_element_type=jnp.float32)
    return dot(high, high_table) + dot(low, high_table) + dot(high, low_table)


def forward_stage(fields, twist, turned, blocks):
    count = fields.shape[0]
    for field in range(count):
        slabs = [fields[field, :, tile(m)] for m in range(blocks // 2)]
        for k, (real, imag) in enumerate(half_circle_forward(slabs)):
            at = pl.ds((k * count + field) * ROWS, ROWS)
            cos, sin = twist[2 * k : 2 * k + 1, :], twist[2 * k + 1 : 2 * k + 2, :]
            if imag is None:
                turned[at, tile(0)] = real * cos
                turned[at, tile(1)] = real * sin
            else:
                turned[at, tile(0)] = real * cos - imag * sin
                turned[at, tile(1)] = real * sin + imag * cos


def own_kernel(blocks, fields, twist, masks, high, low, spectrum, turned):
    kept = blocks // 2 + 1
    forward_stage(fields, twist, turned, blocks)
    result = triple_product(turned[...], high[...], low[...])
    for k in range(kept):
        at = k * 3 * ROWS
        spectrum[at : at + 3 * ROWS, :] = (
            result[at : at + 3 * ROWS, :] * masks[3 * k : 3 * k + 1, :]
        )


def halo_rows(pack, lat_count, field, index):
    if field < 2:
        return pack[HALO * field : HALO * field + HALO, tile(index)]
    last = pack[index // 2 : index // 2 + 1, pl.ds(lat_count + index % 2 * RADIX, RADIX)]
    return jnp.concatenate([pack[2 * HALO : ROWS, tile(index)], last], 0)


def pack_rows(pack, lat_count, field, index, rows):
    if field < 2:
        pack[HALO * field : HALO * field + HALO, tile(index)] = rows
    else:
        pack[2 * HALO : ROWS, tile(index)] = rows[: ROWS - 2 * HALO]
        pack[index // 2 : index // 2 + 1, pl.ds(lat_count + index % 2 * RADIX, RADIX)] = rows[
            ROWS - 2 * HALO :
        ]


def pack_kernel(first_half, second_half, first_pack, last_pack):
    lat_count = first_half.shape[-1]
    for field in range(3):
        for index in range(lat_count // RADIX):
            pack_rows(first_pack, lat_count, field, index, first_half[field, :HALO, tile(index)])
            pack_rows(
                last_pack, lat_count, field, index, second_half[field, ROWS - HALO :, tile(index)]
            )


def step_kernel(
    blocks,
    half,
    final,
    mine,
    other,
    halo,
    far,
    above,
    below,
    spectrum,
    twist,
    back,
    masks,
    rows,
    forward_high,
    forward_low,
    inverse_high,
    inverse_low,
    *rest,
):
    kept = blocks // 2 + 1
    tiles = blocks // 2
    lat_count = mine.shape[-1]
    outs, (turned, weighted, spread, smooth, slope) = rest[:-5], rest[-5:]
    forward_stage(far, twist, turned, blocks)
    result = triple_product(turned[...], forward_high[...], forward_low[...])
    for k in range(kept):
        for field in range(3):
            at = (k * 3 + field) * ROWS
            row = 3 * k + (1 if SIGNS[field] > 0 else 2)
            weighted[at : at + ROWS, :] = (
                spectrum[at : at + ROWS, :] + result[at : at + ROWS, :] * masks[row : row + 1, :]
            )
    spread[...] = triple_product(weighted[...], inverse_high[...], inverse_low[...])
    for field in range(3):
        smooth_terms, slope_terms = [], []
        for k in range(kept):
            at = pl.ds((k * 3 + field) * ROWS, ROWS)
            real, imag, slope_real, slope_imag = [spread[at, tile(i)] for i in range(4)]
            cos, sin, slope_cos, slope_sin = [back[4 * k + i : 4 * k + i + 1, :] for i in range(4)]
            turn_real = real * cos - imag * sin
            turn_imag = real * sin + imag * cos
            wave = 2.0 * math.pi * k / (2 * lat_count)
            smooth_terms.append((turn_real, turn_imag))
            slope_terms.append(
                (
                    slope_real * slope_cos - slope_imag * slope_sin - wave * turn_imag,
                    slope_real * slope_sin + slope_imag * slope_cos + wave * turn_real,
                )
            )
        for m, value in enumerate(half_circle_inverse(smooth_terms)):
            smooth[field, :, tile(m)] = value
        for m, value in enumerate(half_circle_inverse(slope_terms)):
            slope[field, :, tile(m)] = value
    for index in range(tiles):
        zonal = []
        for field in range(3):
            here = mine[field, :, tile(index)]
            edge = halo_rows(halo, lat_count, field, index)
            there = other[field, :, tile(index)]
            if half == 0:
                line = jnp.concatenate([edge, here, there[:HALO]], 0)
            else:
                line = jnp.concatenate([there[ROWS - HALO :], here, edge], 0)
            at = [line[i : i + ROWS] for i in range(2 * HALO + 1)]
            zonal.append(
                (45.0 / 60.0) * (at[4] - at[2])
                - (9.0 / 60.0) * (at[5] - at[1])
                + (1.0 / 60.0) * (at[6] - at[0])
            )
        height, east, north = [mine[field, :, tile(index)] for field in range(3)]
        secant, turning = rows[0:1, tile(index)], rows[1:2, tile(index)]
        low_row = half * ROWS
        vertical = (
            above[low_row : low_row + ROWS, tile(index)]
            + below[low_row : low_row + ROWS, tile(index)]
            - 2.0 * height
        )
        zonal = [secant * value for value in zonal]
        slopes = [slope[field, :, tile(index)] for field in range(3)]
        advect = [east * zonal[field] + north * slopes[field] for field in range(3)]
        tendency = [
            mixing * vertical - advect[0] - height * (zonal[1] + slopes[2]),
            turning * north - advect[1] - zonal[0],
            -advect[2] - slopes[0] - turning * east,
        ]
        values = [smooth[field, :, tile(index)] + courant * tendency[field] for field in range(3)]
        if final:
            for field in range(3):
                outs[0][field, :, tile(index)] = values[field]
        else:
            for field in range(3):
                outs[0][field, :, tile(index)] = values[field]
                chosen = values[field][:HALO] if half == 0 else values[field][ROWS - HALO :]
                pack_rows(outs[1], lat_count, field, index, chosen)


def vmem(count):
    return [pl.BlockSpec(memory_space=pltpu.VMEM)] * count


def params():
    return pltpu.CompilerParams(vmem_limit_bytes=24 * 1024 * 1024)


def shift(value, axis, step, wrap):
    size = lax.axis_size(axis)
    pairs = [(i, (i + step) % size) for i in range(size) if wrap or 0 <= i + step < size]
    return lax.ppermute(value, axis, pairs)


def from_antipode(value):
    size = lax.axis_size("lon")
    return lax.ppermute(value, "lon", [(i, (i + size // 2) % size) for i in range(size)])


def body(thickness, wind_field):
    level_count, lon_count, lat_count = thickness.shape
    assert level_count == 1 and lon_count == 2 * ROWS
    blocks = 2 * lat_count // RADIX
    kept = blocks // 2 + 1
    spectral_rows = (3 * kept * ROWS + 15) // 16 * 16
    forward, inverse, twist, back, masks, rows = numpy_tables(lat_count)
    forward_tables = split_table(forward)
    inverse_tables = split_table(inverse)
    twist, back, masks, rows = [jnp.asarray(a) for a in (twist, back, masks, rows)]
    f32 = jnp.float32
    half_shape = jax.ShapeDtypeStruct((3, ROWS, lat_count), f32)
    pack_shape = jax.ShapeDtypeStruct((ROWS, lat_count + lat_count // ROWS), f32)
    spectrum_shape = jax.ShapeDtypeStruct((spectral_rows, 2 * RADIX), f32)
    scratch = lambda *shape: pltpu.VMEM(shape, f32)

    own = pl.pallas_call(
        functools.partial(own_kernel, blocks),
        out_shape=spectrum_shape,
        in_specs=vmem(5),
        out_specs=vmem(1)[0],
        scratch_shapes=[scratch(spectral_rows, 2 * RADIX)],
        compiler_params=params(),
        name="own_spectrum",
    )
    pack = pl.pallas_call(
        pack_kernel,
        out_shape=[pack_shape] * 2,
        in_specs=vmem(2),
        out_specs=vmem(2),
        compiler_params=params(),
        name="pack_halo",
    )

    def advance(half, final, *args):
        outs = [half_shape] if final else [half_shape, pack_shape]
        return pl.pallas_call(
            functools.partial(step_kernel, blocks, half, final),
            out_shape=outs,
            in_specs=vmem(len(args)),
            out_specs=vmem(len(outs)),
            scratch_shapes=[
                scratch(spectral_rows, 2 * RADIX),
                scratch(spectral_rows, 2 * RADIX),
                scratch(spectral_rows, 4 * RADIX),
                scratch(3, ROWS, lat_count),
                scratch(3, ROWS, lat_count),
            ],
            compiler_params=params(),
            name=f"advance_half",
        )(*args)

    fields = jnp.concatenate([thickness, wind_field[:, 0]], 0)
    halves = [fields[:, :ROWS], fields[:, ROWS:]]
    packs = None
    height = thickness[0]
    for step in range(STEPS):
        final = step == STEPS - 1
        far = [from_antipode(half) for half in halves]
        spectra = [own(half, twist, masks, *forward_tables) for half in halves]
        if packs is None:
            packs = pack(*halves)
        first_pack, last_pack = packs
        halo_left = shift(last_pack, "lon", 1, True)
        halo_right = shift(first_pack, "lon", -1, True)
        above = shift(height, "lev", -1, False)
        below = shift(height, "lev", 1, False)
        results = []
        for half in range(2):
            results.append(
                advance(
                    half,
                    final,
                    halves[half],
                    halves[1 - half],
                    (halo_left, halo_right)[half],
                    far[half],
                    above,
                    below,
                    spectra[half],
                    twist,
                    back,
                    masks,
                    rows,
                    *forward_tables,
                    *inverse_tables,
                )
            )
        halves = [result[0] for result in results]
        if not final:
            packs = [result[1] for result in results]
            height = jnp.concatenate([half[0] for half in halves], 0)
    fields = jnp.concatenate(halves, 1)
    return fields[:1], fields[1:, None]


def solution(mesh):
    in_specs = (P("lev", "lon", None), P(None, "lev", "lon", None))
    out_specs = (P("lev", "lon", None), P(None, "lev", "lon", None))
    return jax.shard_map(body, mesh=mesh, in_specs=in_specs, out_specs=out_specs, check_vma=False)
```

```python
import functools
import math

import jax
import jax.numpy as jnp
import numpy as np
from jax import lax
from jax.experimental import pallas as pl
from jax.experimental.pallas import tpu as pltpu
from jax.sharding import PartitionSpec as P

STEPS = 2

courant = 0.2
mixing = 0.25
coriolis = 0.5
cos_floor = 0.25

RADIX = 128
ROWS = 8
TRANSFORM_COST = 10_000_000_000
PIECES = 4
HALO = 3


def split_table(table):
    high = table.astype(np.float32).astype(jnp.bfloat16)
    low = (table - high.astype(np.float64)).astype(np.float32).astype(jnp.bfloat16)
    return jnp.asarray(high), jnp.asarray(low)


@functools.lru_cache(maxsize=None)
def numpy_tables(lat_count):
    length = 2 * lat_count
    blocks = length // RADIX
    kept = blocks // 2 + 1
    centred = np.arange(RADIX) + 0.5
    order = np.arange(RADIX)
    signed = np.where(order < RADIX // 2, order, order - RADIX).astype(np.float64)
    angle = 2.0 * np.pi / RADIX * centred[:, None] * signed[None, :]
    cos, sin = np.cos(angle), np.sin(angle)
    forward = np.block([[cos, -sin], [sin, cos]])
    cos_t, sin_t = cos.T, sin.T
    weight = signed[:, None]
    inverse = np.block(
        [
            [cos_t, sin_t, -weight * sin_t, weight * cos_t],
            [-sin_t, cos_t, -weight * cos_t, -weight * sin_t],
        ]
    )
    first = np.arange(kept)
    turn = 2.0 * np.pi / length * first[:, None] * centred[None, :]
    twist = np.stack([np.cos(turn), -np.sin(turn)], 1)
    share = np.where((first == 0) | (first == blocks // 2), 1.0, 2.0)[:, None] / length
    back = np.stack([np.cos(turn) * share, np.sin(turn) * share], 1)
    slope_scale = 2.0 * np.pi * blocks / length
    back = np.concatenate([back, back * slope_scale], 1)
    wave = first[:, None] + blocks * signed[None, :]
    retained = (np.abs(wave) <= length // 3).astype(np.float64)
    plus = np.concatenate([retained, retained], 1)
    minus = np.concatenate([retained, -retained], 1)
    masks = np.stack([plus, minus, -minus], 1)
    latitude = (np.arange(lat_count) + 0.5) * (np.pi / lat_count) - 0.5 * np.pi
    rows = np.stack(
        [1.0 / np.maximum(np.cos(latitude), cos_floor), coriolis * np.sin(latitude)]
    )
    flat = lambda a: a.reshape(-1, a.shape[-1]).astype(np.float32)
    return forward, inverse, flat(twist), flat(back), flat(masks), rows.astype(np.float32)


def times(value, angle):
    real, imag = value
    cos, sin = math.cos(angle), math.sin(angle)
    quarter = round(angle / (math.pi / 2), 9)
    if quarter == int(quarter):
        turn = int(quarter) % 4
        return [(real, imag), (-imag, real), (-real, -imag), (imag, -real)][turn]
    if abs(abs(cos) - abs(sin)) < 1e-12:
        scale = abs(cos)
        a = real if cos > 0 else -real
        b = imag if cos > 0 else -imag
        c = imag if sin > 0 else -imag
        d = real if sin > 0 else -real
        return (scale * (a - c), scale * (b + d))
    return (real * cos - imag * sin, imag * cos + real * sin)


def add(a, b):
    return (a[0] + b[0], a[1] + b[1])


def sub(a, b):
    return (a[0] - b[0], a[1] - b[1])


def complex_dft(values, sign):
    n = len(values)
    if n == 1:
        return values
    half = n // 2
    even = complex_dft([add(values[m], values[m + half]) for m in range(half)], sign)
    odd = complex_dft(
        [
            times(sub(values[m], values[m + half]), sign * 2 * math.pi * m / n)
            for m in range(half)
        ],
        sign,
    )
    return [even[q // 2] if q % 2 == 0 else odd[q // 2] for q in range(n)]


def odd_outputs(values):
    r = len(values)
    if r == 1:
        return {1: (values[0], None)}
    half = r // 2
    turned = [
        times((values[m], -values[m + half]), -math.pi * m / r) for m in range(half)
    ]
    out = {}
    for q, value in enumerate(complex_dft(turned, -1)):
        j = 4 * q + 1
        out[j if j <= r else 2 * r - j] = value if j <= r else (value[0], -value[1])
    return out


def half_circle_forward(values):
    n = len(values)
    out = {j: value for j, value in odd_outputs(values).items()}
    scale = 2
    while len(values) > 1:
        half = len(values) // 2
        difference = [values[m] - values[m + half] for m in range(half)]
        values = [values[m] + values[m + half] for m in range(half)]
        for j, value in odd_outputs(difference).items():
            out[j * scale] = value
        scale *= 2
    out[0] = (values[0], None)
    return [out[k] for k in range(n + 1)]


def odd_inputs(values, r):
    if r == 1:
        return [values[1][0]]
    half = r // 2
    gathered = []
    for q in range(half):
        j = 4 * q + 1
        if j <= r:
            gathered.append(values[j])
        else:
            real, imag = values[2 * r - j]
            gathered.append((real, -imag))
    turned = [
        times(value, math.pi * m / r) for m, value in enumerate(complex_dft(gathered, 1))
    ]
    return [value[0] for value in turned] + [-value[1] for value in turned]


def half_circle_inverse(values):
    n = len(values) - 1
    result = [values[0][0]]
    size = 1
    while size < n:
        step = n // size
        difference = odd_inputs({j: values[j * step] for j in range(1, size + 1, 2)}, size)
        result = [result[m] + difference[m] for m in range(size)] + [
            result[m] - difference[m] for m in range(size)
        ]
        size *= 2
    last = odd_inputs({j: values[j] for j in range(1, n + 1, 2)}, n)
    return [result[m] + last[m] for m in range(n)]


def tile(index):
    return pl.ds(index * RADIX, RADIX)


def split(value):
    high = value.astype(jnp.bfloat16)
    return high, (value - high.astype(jnp.float32)).astype(jnp.bfloat16)


def triple_product(value, high_table, low_table):
    high, low = split(value)
    dot = functools.partial(jnp.dot, preferred_element_type=jnp.float32)
    return dot(high, high_table) + dot(low, high_table) + dot(high, low_table)


def forward_stage(slabs_of, groups, twist, turned, blocks):
    for group in range(groups):
        slabs = slabs_of(group)
        for k, (real, imag) in enumerate(half_circle_forward(slabs)):
            at = pl.ds((k * groups + group) * ROWS, ROWS)
            cos, sin = twist[2 * k : 2 * k + 1, :], twist[2 * k + 1 : 2 * k + 2, :]
            if imag is None:
                turned[at, tile(0)] = real * cos
                turned[at, tile(1)] = real * sin
            else:
                turned[at, tile(0)] = real * cos - imag * sin
                turned[at, tile(1)] = real * sin + imag * cos


def reader(fields, tiles):
    per_field = fields.shape[1] // ROWS

    def slabs_of(group):
        field, part = divmod(group, per_field)
        return [fields[field, part * ROWS : part * ROWS + ROWS, tile(m)] for m in range(tiles)]

    return slabs_of


def pack_rows(pack, lat_count, field, index, rows):
    if field < 2:
        pack[HALO * field : HALO * field + HALO, tile(index)] = rows
    else:
        pack[2 * HALO : ROWS, tile(index)] = rows[: ROWS - 2 * HALO]
        pack[index // 2 : index // 2 + 1, pl.ds(lat_count + index % 2 * RADIX, RADIX)] = rows[
            ROWS - 2 * HALO :
        ]


def halo_rows(pack, lat_count, field, index):
    if field < 2:
        return pack[HALO * field : HALO * field + HALO, tile(index)]
    last = pack[index // 2 : index // 2 + 1, pl.ds(lat_count + index % 2 * RADIX, RADIX)]
    return jnp.concatenate([pack[2 * HALO : ROWS, tile(index)], last], 0)


def field_of(height, wind, field, index):
    return height[0, :, tile(index)] if field == 0 else wind[field - 1, :, tile(index)]


def odd_device():
    return lax.rem(lax.axis_index("lon"), 2) == 1


def pack_edge(height, wind, pack, first):
    lat_count = height.shape[-1]
    for field in range(3):
        for index in range(lat_count // RADIX):
            rows = field_of(height, wind, field, index)
            chosen = jnp.where(first, rows[:HALO], rows[rows.shape[0] - HALO :])
            pack_rows(pack, lat_count, field, index, chosen)


def gather_kernel(fields, height, wind, near_pack):
    height[...] = fields[:1]
    wind[...] = fields[1:]
    pack_edge(height, wind, near_pack, odd_device())


def own_kernel(blocks, near, height, wind, twist, masks, high, low, *rest):
    spectra, (far_pack, height_copy), turned = rest[:2], rest[2:4], rest[4:]
    pack_edge(height, wind, far_pack, jnp.logical_not(odd_device()))
    height_copy[...] = height[...]
    kept = blocks // 2 + 1
    for fields, spectrum, work in zip((height, wind), spectra, turned):
        span = fields.shape[0] * fields.shape[1]
        forward_stage(reader(fields, blocks // 2), span // ROWS, twist, work, blocks)
        result = triple_product(work[...], high[...], low[...])
        for k in range(kept):
            at = k * span
            spectrum[at : at + span, :] = result[at : at + span, :] * masks[3 * k : 3 * k + 1, :]


def far_kernel(
    blocks,
    parity,
    far,
    spectrum,
    twist,
    back,
    masks,
    forward_high,
    forward_low,
    inverse_high,
    inverse_low,
    *rest,
):
    smooth, slope, turned, weighted, spread = rest[-5:]
    kept = blocks // 2 + 1
    tiles = blocks // 2
    count, lon_count = far.shape[:2]
    per_field = lon_count // ROWS
    groups = count * per_field
    length = blocks * RADIX
    forward_stage(reader(far, tiles), groups, twist, turned, blocks)
    result = triple_product(turned[...], forward_high[...], forward_low[...])
    span = groups * ROWS
    for k in range(kept):
        at = k * span
        row = 3 * k + (1 if parity > 0 else 2)
        weighted[at : at + span, :] = (
            spectrum[at : at + span, :] + result[at : at + span, :] * masks[row : row + 1, :]
        )
    spread[...] = triple_product(weighted[...], inverse_high[...], inverse_low[...])
    for group in range(groups):
        field, part = divmod(group, per_field)
        out = slice(part * ROWS, part * ROWS + ROWS)
        smooth_terms, slope_terms = [], []
        for k in range(kept):
            at = pl.ds((k * groups + group) * ROWS, ROWS)
            real, imag, slope_real, slope_imag = [spread[at, tile(i)] for i in range(4)]
            cos, sin, slope_cos, slope_sin = [back[4 * k + i : 4 * k + i + 1, :] for i in range(4)]
            turn_real = real * cos - imag * sin
            turn_imag = real * sin + imag * cos
            wave = 2.0 * math.pi * k / length
            smooth_terms.append((turn_real, turn_imag))
            slope_terms.append(
                (
                    slope_real * slope_cos - slope_imag * slope_sin - wave * turn_imag,
                    slope_real * slope_sin + slope_imag * slope_cos + wave * turn_real,
                )
            )
        for m, value in enumerate(half_circle_inverse(smooth_terms)):
            smooth[field, out, tile(m)] = value
        for m, value in enumerate(half_circle_inverse(slope_terms)):
            slope[field, out, tile(m)] = value


def update_kernel(
    final,
    height,
    wind,
    near,
    far,
    first_level,
    second_level,
    height_smooth,
    height_slope,
    wind_smooth,
    wind_slope,
    rows,
    *outs,
):
    lon_count, lat_count = height.shape[1:]
    tiles = lat_count // RADIX
    odd = odd_device()
    if final:
        height_out, wind_out, staged, sems = outs
    copies = []
    for index in range(tiles):
        here = [field_of(height, wind, field, index) for field in range(3)]
        zonal = []
        for field in range(3):
            close = halo_rows(near, lat_count, field, index)
            away = halo_rows(far, lat_count, field, index)
            line = jnp.concatenate(
                [jnp.where(odd, close, away), here[field], jnp.where(odd, away, close)], 0
            )
            at = [line[i : i + lon_count] for i in range(2 * HALO + 1)]
            zonal.append(
                (45.0 / 60.0) * (at[4] - at[2])
                - (9.0 / 60.0) * (at[5] - at[1])
                + (1.0 / 60.0) * (at[6] - at[0])
            )
        thick, east, north = here
        secant, turning = rows[0:1, tile(index)], rows[1:2, tile(index)]
        vertical = first_level[0, :, tile(index)] + second_level[0, :, tile(index)] - 2.0 * thick
        zonal = [secant * value for value in zonal]
        slopes = [
            height_slope[0, :, tile(index)],
            wind_slope[0, :, tile(index)],
            wind_slope[1, :, tile(index)],
        ]
        smooths = [
            height_smooth[0, :, tile(index)],
            wind_smooth[0, :, tile(index)],
            wind_smooth[1, :, tile(index)],
        ]
        advect = [east * zonal[field] + north * slopes[field] for field in range(3)]
        tendency = [
            mixing * vertical - advect[0] - thick * (zonal[1] + slopes[2]),
            turning * north - advect[1] - zonal[0],
            -advect[2] - slopes[0] - turning * east,
        ]
        values = [smooths[field] + courant * tendency[field] for field in range(3)]
        if final:
            for field in range(3):
                staged[field, :, tile(index)] = values[field]
            if (index + 1) % (tiles // PIECES) == 0:
                piece = (index + 1) // (tiles // PIECES) - 1
                at = pl.ds(piece * (lat_count // PIECES), lat_count // PIECES)
                for field in range(3):
                    target = (
                        height_out.at[0, :, at] if field == 0 else wind_out.at[field - 1, :, at]
                    )
                    copy = pltpu.make_async_copy(
                        staged.at[field, :, at], target, sems.at[piece * 3 + field]
                    )
                    copy.start()
                    copies.append(copy)
        else:
            height_next, wind_next, near_pack = outs
            height_next[0, :, tile(index)] = values[0]
            for field in range(1, 3):
                wind_next[field - 1, :, tile(index)] = values[field]
            for field in range(3):
                first, last = values[field][:HALO], values[field][lon_count - HALO :]
                pack_rows(near_pack, lat_count, field, index, jnp.where(odd, first, last))
    for copy in copies:
        copy.wait()


def vmem(count):
    return [pl.BlockSpec(memory_space=pltpu.VMEM)] * count


def anywhere(count):
    return [pl.BlockSpec(memory_space=pl.ANY)] * count


def params():
    return pltpu.CompilerParams(vmem_limit_bytes=24 * 1024 * 1024)


def exchange(value, axis, first):
    size = lax.axis_size(axis)
    wrap = axis == "lon"
    pairs = [(i, (i + 1) % size) for i in range(first, size if wrap else size - 1, 2)]
    return lax.ppermute(value, axis, pairs + [(j, i) for i, j in pairs])


def from_antipode(value):
    size = lax.axis_size("lon")
    return lax.ppermute(value, "lon", [(i, (i + size // 2) % size) for i in range(size)])


def body(thickness, wind_field):
    level_count, lon_count, lat_count = thickness.shape
    assert level_count == 1 and lon_count % ROWS == 0
    blocks = 2 * lat_count // RADIX
    kept = blocks // 2 + 1
    forward, inverse, twist, back, masks, rows = numpy_tables(lat_count)
    forward_tables = split_table(forward)
    inverse_tables = split_table(inverse)
    twist, back, masks, rows = [jnp.asarray(a) for a in (twist, back, masks, rows)]
    f32 = jnp.float32
    array = lambda *shape: jax.ShapeDtypeStruct(shape, f32)
    scratch = lambda *shape: pltpu.VMEM(shape, f32)
    height_shape, wind_shape = array(1, lon_count, lat_count), array(2, lon_count, lat_count)
    pack_shape = array(ROWS, lat_count + lat_count // ROWS)
    spectral = lambda count, width: (count * kept * lon_count, width * RADIX)

    def call(kernel, name, outs, scratches, *args, in_specs=None, out_specs=None, cost=None):
        return pl.pallas_call(
            kernel,
            out_shape=outs,
            in_specs=in_specs or vmem(len(args)),
            out_specs=out_specs or vmem(len(outs)),
            scratch_shapes=scratches,
            compiler_params=params(),
            cost_estimate=cost
            and pl.CostEstimate(flops=cost, bytes_accessed=cost // 300, transcendentals=0),
            name=name,
        )(*args)

    def transform(count, parity, far, spectrum, *after):
        return call(
            functools.partial(far_kernel, blocks, parity),
            "antipode_transform",
            [array(count, lon_count, lat_count)] * 2,
            [scratch(*spectral(count, 2))] * 2 + [scratch(*spectral(count, 4))],
            far,
            spectrum,
            twist,
            back,
            masks,
            *forward_tables,
            *inverse_tables,
            *after,
            in_specs=vmem(9) + anywhere(len(after)),
            cost=TRANSFORM_COST,
        )

    far_wind = from_antipode(wind_field.reshape(wind_shape.shape))
    far_height = from_antipode(thickness)
    moving = [height_shape, wind_shape, pack_shape]
    fields = jnp.concatenate([thickness, wind_field.reshape(wind_shape.shape)], 0)
    height, wind, near_pack = call(gather_kernel, "gather_fields", moving, [], fields)
    for step in range(STEPS):
        near = exchange(near_pack, "lon", 0)
        height_spectrum, wind_spectrum, far_pack, height_copy = call(
            functools.partial(own_kernel, blocks),
            "own_spectra",
            [array(*spectral(1, 2)), array(*spectral(2, 2)), pack_shape, height_shape],
            [scratch(*spectral(1, 2)), scratch(*spectral(2, 2))],
            near,
            height,
            wind,
            twist,
            masks,
            *forward_tables,
            in_specs=anywhere(1) + vmem(6),
        )
        levels = [exchange(height_copy, "lev", first) for first in (0, 1)]
        far = exchange(far_pack, "lon", 1)
        wind_terms = transform(2, -1, far_wind, wind_spectrum)
        height_terms = transform(1, 1, far_height, height_spectrum, wind_terms[0])
        args = (height, wind, near, far, *levels, *height_terms, *wind_terms, rows)
        if step == STEPS - 1:
            height, wind = call(
                functools.partial(update_kernel, True),
                "update_fields",
                [height_shape, wind_shape],
                [scratch(3, lon_count, lat_count), pltpu.SemaphoreType.DMA((3 * PIECES,))],
                *args,
                out_specs=anywhere(2),
            )
            return height, wind.reshape(wind_field.shape)
        height, wind, near_pack = call(
            functools.partial(update_kernel, False),
            "update_fields",
            moving,
            [],
            *args,
        )
        far_wind, far_height = from_antipode(wind), from_antipode(height)


def solution(mesh):
    in_specs = (P("lev", "lon", None), P(None, "lev", "lon", None))
    out_specs = (P("lev", "lon", None), P(None, "lev", "lon", None))
    return jax.shard_map(body, mesh=mesh, in_specs=in_specs, out_specs=out_specs, check_vma=False)
```

```python
import functools
import math

import jax
import jax.numpy as jnp
import numpy as np
from jax import lax
from jax.experimental import pallas as pl
from jax.experimental.pallas import tpu as pltpu
from jax.sharding import PartitionSpec as P

STEPS = 2

courant = 0.2
mixing = 0.25
coriolis = 0.5
cos_floor = 0.25

RADIX = 128
ROWS = 8
FIRST_COST = 2000000000
SECOND_COST = 2000000000
PIECES = 4
HALO = 3


def split_table(table):
    high = table.astype(np.float32).astype(jnp.bfloat16)
    low = (table - high.astype(np.float64)).astype(np.float32).astype(jnp.bfloat16)
    return jnp.asarray(high), jnp.asarray(low)


@functools.lru_cache(maxsize=None)
def numpy_tables(lat_count):
    length = 2 * lat_count
    blocks = length // RADIX
    kept = blocks // 2 + 1
    centred = np.arange(RADIX) + 0.5
    order = np.arange(RADIX)
    signed = np.where(order < RADIX // 2, order, order - RADIX).astype(np.float64)
    angle = 2.0 * np.pi / RADIX * centred[:, None] * signed[None, :]
    cos, sin = np.cos(angle), np.sin(angle)
    forward = np.block([[cos, -sin], [sin, cos]])
    cos_t, sin_t = cos.T, sin.T
    weight = signed[:, None]
    inverse = np.block(
        [
            [cos_t, sin_t, -weight * sin_t, weight * cos_t],
            [-sin_t, cos_t, -weight * cos_t, -weight * sin_t],
        ]
    )
    first = np.arange(kept)
    turn = 2.0 * np.pi / length * first[:, None] * centred[None, :]
    twist = np.stack([np.cos(turn), -np.sin(turn)], 1)
    share = np.where((first == 0) | (first == blocks // 2), 1.0, 2.0)[:, None] / length
    back = np.stack([np.cos(turn) * share, np.sin(turn) * share], 1)
    slope_scale = 2.0 * np.pi * blocks / length
    back = np.concatenate([back, back * slope_scale], 1)
    wave = first[:, None] + blocks * signed[None, :]
    retained = (np.abs(wave) <= length // 3).astype(np.float64)
    plus = np.concatenate([retained, retained], 1)
    minus = np.concatenate([retained, -retained], 1)
    masks = np.stack([plus, minus, -minus], 1)
    latitude = (np.arange(lat_count) + 0.5) * (np.pi / lat_count) - 0.5 * np.pi
    rows = np.stack(
        [1.0 / np.maximum(np.cos(latitude), cos_floor), coriolis * np.sin(latitude)]
    )
    flat = lambda a: a.reshape(-1, a.shape[-1]).astype(np.float32)
    return forward, inverse, flat(twist), flat(back), flat(masks), rows.astype(np.float32)


def times(value, angle):
    real, imag = value
    cos, sin = math.cos(angle), math.sin(angle)
    quarter = round(angle / (math.pi / 2), 9)
    if quarter == int(quarter):
        turn = int(quarter) % 4
        return [(real, imag), (-imag, real), (-real, -imag), (imag, -real)][turn]
    if abs(abs(cos) - abs(sin)) < 1e-12:
        scale = abs(cos)
        a = real if cos > 0 else -real
        b = imag if cos > 0 else -imag
        c = imag if sin > 0 else -imag
        d = real if sin > 0 else -real
        return (scale * (a - c), scale * (b + d))
    return (real * cos - imag * sin, imag * cos + real * sin)


def add(a, b):
    return (a[0] + b[0], a[1] + b[1])


def sub(a, b):
    return (a[0] - b[0], a[1] - b[1])


def complex_dft(values, sign):
    n = len(values)
    if n == 1:
        return values
    half = n // 2
    even = complex_dft([add(values[m], values[m + half]) for m in range(half)], sign)
    odd = complex_dft(
        [
            times(sub(values[m], values[m + half]), sign * 2 * math.pi * m / n)
            for m in range(half)
        ],
        sign,
    )
    return [even[q // 2] if q % 2 == 0 else odd[q // 2] for q in range(n)]


def odd_outputs(values):
    r = len(values)
    if r == 1:
        return {1: (values[0], None)}
    half = r // 2
    turned = [
        times((values[m], -values[m + half]), -math.pi * m / r) for m in range(half)
    ]
    out = {}
    for q, value in enumerate(complex_dft(turned, -1)):
        j = 4 * q + 1
        out[j if j <= r else 2 * r - j] = value if j <= r else (value[0], -value[1])
    return out


def half_circle_forward(values):
    n = len(values)
    out = {j: value for j, value in odd_outputs(values).items()}
    scale = 2
    while len(values) > 1:
        half = len(values) // 2
        difference = [values[m] - values[m + half] for m in range(half)]
        values = [values[m] + values[m + half] for m in range(half)]
        for j, value in odd_outputs(difference).items():
            out[j * scale] = value
        scale *= 2
    out[0] = (values[0], None)
    return [out[k] for k in range(n + 1)]


def odd_inputs(values, r):
    if r == 1:
        return [values[1][0]]
    half = r // 2
    gathered = []
    for q in range(half):
        j = 4 * q + 1
        if j <= r:
            gathered.append(values[j])
        else:
            real, imag = values[2 * r - j]
            gathered.append((real, -imag))
    turned = [
        times(value, math.pi * m / r) for m, value in enumerate(complex_dft(gathered, 1))
    ]
    return [value[0] for value in turned] + [-value[1] for value in turned]


def half_circle_inverse(values):
    n = len(values) - 1
    result = [values[0][0]]
    size = 1
    while size < n:
        step = n // size
        difference = odd_inputs({j: values[j * step] for j in range(1, size + 1, 2)}, size)
        result = [result[m] + difference[m] for m in range(size)] + [
            result[m] - difference[m] for m in range(size)
        ]
        size *= 2
    last = odd_inputs({j: values[j] for j in range(1, n + 1, 2)}, n)
    return [result[m] + last[m] for m in range(n)]


def tile(index):
    return pl.ds(index * RADIX, RADIX)


def split(value):
    high = value.astype(jnp.bfloat16)
    return high, (value - high.astype(jnp.float32)).astype(jnp.bfloat16)


def triple_product(value, high_table, low_table):
    high, low = split(value)
    left = jnp.concatenate([high, low, high], 1)
    right = jnp.concatenate([high_table, high_table, low_table], 0)
    return jnp.dot(left, right, preferred_element_type=jnp.float32)


def forward_stage(slabs_of, groups, twist, turned, blocks):
    for group in range(groups):
        slabs = slabs_of(group)
        for k, (real, imag) in enumerate(half_circle_forward(slabs)):
            at = pl.ds((k * groups + group) * ROWS, ROWS)
            cos, sin = twist[2 * k : 2 * k + 1, :], twist[2 * k + 1 : 2 * k + 2, :]
            if imag is None:
                turned[at, tile(0)] = real * cos
                turned[at, tile(1)] = real * sin
            else:
                turned[at, tile(0)] = real * cos - imag * sin
                turned[at, tile(1)] = real * sin + imag * cos


def row_groups(lon_count):
    return [slice(i, i + ROWS) for i in range(0, lon_count, ROWS)]


def pack_rows(pack, lat_count, field, index, rows):
    if field < 2:
        pack[HALO * field : HALO * field + HALO, tile(index)] = rows
    else:
        pack[2 * HALO : ROWS, tile(index)] = rows[: ROWS - 2 * HALO]
        pack[index // 2 : index // 2 + 1, pl.ds(lat_count + index % 2 * RADIX, RADIX)] = rows[
            ROWS - 2 * HALO :
        ]


def halo_rows(pack, lat_count, field, index):
    if field < 2:
        return pack[HALO * field : HALO * field + HALO, tile(index)]
    last = pack[index // 2 : index // 2 + 1, pl.ds(lat_count + index % 2 * RADIX, RADIX)]
    return jnp.concatenate([pack[2 * HALO : ROWS, tile(index)], last], 0)


def field_at(east, rest, field, *at):
    return east[(0, *at)] if field == 0 else rest[(field - 1, *at)]


def odd_device():
    return lax.rem(lax.axis_index("lon"), 2) == 1


def pack_tile(field, index, rows, near_pack, far_pack, lat_count):
    first, last = rows[:HALO], rows[rows.shape[0] - HALO :]
    odd = odd_device()
    pack_rows(near_pack, lat_count, field, index, jnp.where(odd, first, last))
    pack_rows(far_pack, lat_count, field, index, jnp.where(odd, last, first))


def gather_kernel(fields, east, rest, height, near_pack, far_pack):
    lat_count = fields.shape[-1]
    for index in range(lat_count // RADIX):
        at = tile(index)
        thickness, eastward, northward = [fields[i, :, at] for i in range(3)]
        east[0, :, at] = eastward
        rest[0, :, at] = northward
        rest[1, :, at] = thickness
        height[0, :, at] = thickness
        for field, rows in enumerate((eastward, northward, thickness)):
            pack_tile(field, index, rows, near_pack, far_pack, lat_count)


def own_kernel(blocks, split_at, near, east, rest, twist, masks, high, low, *refs):
    first, second, turned = refs
    kept = blocks // 2 + 1
    lon_count = east.shape[1]
    groups = [(field, at) for field in range(3) for at in row_groups(lon_count)]

    def slabs_of(group):
        field, at = groups[group]
        return [field_at(east, rest, field, at, tile(m)) for m in range(blocks // 2)]

    forward_stage(slabs_of, len(groups), twist, turned, blocks)
    result = triple_product(turned[...], high[...], low[...])
    cut, span = split_at * lon_count, 3 * lon_count
    for k in range(kept):
        value = result[k * span : k * span + span, :] * masks[3 * k : 3 * k + 1, :]
        first[k * cut : k * cut + cut, :] = value[:cut]
        second[k * (span - cut) : (k + 1) * (span - cut), :] = value[cut:]


def transform(blocks, parities, far, spectrum, tables, smooth, slope, work):
    twist, back, masks, forward_high, forward_low, inverse_high, inverse_low = tables
    turned, weighted, spread = work
    kept = blocks // 2 + 1
    count, lon_count = far.shape[:2]
    length = blocks * RADIX
    groups = [(field, at) for field in range(count) for at in row_groups(lon_count)]

    def slabs_of(group):
        field, at = groups[group]
        return [far[field, at, tile(m)] for m in range(blocks // 2)]

    forward_stage(slabs_of, len(groups), twist, turned, blocks)
    result = triple_product(turned[...], forward_high[...], forward_low[...])
    for k in range(kept):
        for field, parity in enumerate(parities):
            at = (k * count + field) * lon_count
            row = 3 * k + (1 if parity > 0 else 2)
            weighted[at : at + lon_count, :] = (
                spectrum[at : at + lon_count, :]
                + result[at : at + lon_count, :] * masks[row : row + 1, :]
            )
    spread[...] = triple_product(weighted[...], inverse_high[...], inverse_low[...])
    for group, (field, out) in enumerate(groups):
        smooth_terms, slope_terms = [], []
        for k in range(kept):
            at = pl.ds((k * len(groups) + group) * ROWS, ROWS)
            real, imag, slope_real, slope_imag = [spread[at, tile(i)] for i in range(4)]
            cos, sin, slope_cos, slope_sin = [back[4 * k + i : 4 * k + i + 1, :] for i in range(4)]
            turn_real = real * cos - imag * sin
            turn_imag = real * sin + imag * cos
            wave = 2.0 * math.pi * k / length
            smooth_terms.append((turn_real, turn_imag))
            slope_terms.append(
                (
                    slope_real * slope_cos - slope_imag * slope_sin - wave * turn_imag,
                    slope_real * slope_sin + slope_imag * slope_cos + wave * turn_real,
                )
            )
        for m, value in enumerate(half_circle_inverse(smooth_terms)):
            smooth[field, out, tile(m)] = value
        for m, value in enumerate(half_circle_inverse(slope_terms)):
            slope[field, out, tile(m)] = value


def first_kernel(blocks, with_north, far_rows, spectrum, east, rest, near, far, rows, *refs):
    tables, refs = refs[:7], refs[7:]
    lon_count, lat_count = east.shape[1:]
    odd = odd_device()
    east_next, zonal_terms = refs[:2]
    if with_north:
        north_terms, refs = refs[2], refs[3:]
    else:
        refs = refs[2:]
    smooth, slope, *work = refs
    count = far_rows.shape[0]
    transform(blocks, (-1,) * count, far_rows, spectrum, tables, smooth, slope, work)
    if with_north:
        north_terms[0] = smooth[1]
        north_terms[1] = slope[1]
    for index in range(lat_count // RADIX):
        here = [field_at(east, rest, field, slice(None), tile(index)) for field in range(3)]
        secant, turning = rows[0:1, tile(index)], rows[1:2, tile(index)]
        zonal = []
        for field in range(3):
            close = halo_rows(near, lat_count, field, index)
            away = halo_rows(far, lat_count, field, index)
            line = jnp.concatenate(
                [jnp.where(odd, close, away), here[field], jnp.where(odd, away, close)], 0
            )
            at = [line[i : i + lon_count] for i in range(2 * HALO + 1)]
            difference = (
                (45.0 / 60.0) * (at[4] - at[2])
                - (9.0 / 60.0) * (at[5] - at[1])
                + (1.0 / 60.0) * (at[6] - at[0])
            )
            zonal.append(secant * difference)
        eastward, northward, thick = here
        tendency = (
            turning * northward
            - eastward * zonal[0]
            - northward * slope[0, :, tile(index)]
            - zonal[2]
        )
        east_next[0, :, tile(index)] = smooth[0, :, tile(index)] + courant * tendency
        zonal_terms[0, :, tile(index)] = -eastward * zonal[1] - turning * eastward
        zonal_terms[1, :, tile(index)] = -eastward * zonal[2] - thick * zonal[0]


def second_kernel(
    blocks, with_north, final, far_rows, spectrum, rest, zonal_terms, *refs
):
    tables, refs = refs[:7], refs[7:]
    if with_north:
        north_terms, refs = refs[0], refs[1:]
    lat_count = rest.shape[-1]
    if final:
        rest_next, *refs = refs
    else:
        (east_next, levels, others, rest_next, height_next, near_pack, far_pack, *refs) = refs
    smooth, slope, *work = refs
    parities = (1,) if with_north else (-1, 1)
    transform(blocks, parities, far_rows, spectrum, tables, smooth, slope, work)
    for index in range(lat_count // RADIX):
        at = tile(index)
        northward, thick = rest[0, :, at], rest[1, :, at]
        last = len(parities) - 1
        thick_smooth, thick_slope = smooth[last, :, at], slope[last, :, at]
        north_smooth = north_terms[0, :, at] if with_north else smooth[0, :, at]
        north_slope = north_terms[1, :, at] if with_north else slope[0, :, at]
        north_tendency = zonal_terms[0, :, at] - northward * north_slope - thick_slope
        thick_tendency = zonal_terms[1, :, at] - northward * thick_slope - thick * north_slope
        if final:
            thick_tendency -= 2.0 * mixing * thick
        else:
            thick_tendency += mixing * (levels[0, :, at] + others[0, :, at] - 2.0 * thick)
        values = (
            north_smooth + courant * north_tendency,
            thick_smooth + courant * thick_tendency,
        )
        for field in range(2):
            rest_next[field, :, at] = values[field]
        if not final:
            height_next[0, :, at] = values[1]
            for field, moved in enumerate((east_next[0, :, at], *values)):
                pack_tile(field, index, moved, near_pack, far_pack, lat_count)


def last_kernel(east, rest, levels, others, height_out, wind_out, height, sems):
    tiles = height.shape[-1] // RADIX
    copies = [
        pltpu.make_async_copy(east.at[0], wind_out.at[0], sems.at[0]),
        pltpu.make_async_copy(rest.at[0], wind_out.at[1], sems.at[1]),
    ]
    for copy in copies:
        copy.start()
    for piece in range(PIECES):
        for index in range(piece * tiles // PIECES, (piece + 1) * tiles // PIECES):
            at = tile(index)
            height[:, at] = rest[1, :, at] + (courant * mixing) * (
                levels[0, :, at] + others[0, :, at]
            )
        span = pl.ds(piece * tiles // PIECES * RADIX, tiles // PIECES * RADIX)
        copies.append(
            pltpu.make_async_copy(height.at[:, span], height_out.at[0, :, span], sems.at[2 + piece])
        )
        copies[-1].start()
    for copy in copies:
        copy.wait()


def vmem(count):
    return [pl.BlockSpec(memory_space=pltpu.VMEM)] * count


def anywhere(count):
    return [pl.BlockSpec(memory_space=pl.ANY)] * count


def params():
    return pltpu.CompilerParams(vmem_limit_bytes=24 * 1024 * 1024)


def exchange(value, axis, first):
    size = lax.axis_size(axis)
    wrap = axis == "lon"
    pairs = [(i, (i + 1) % size) for i in range(first, size if wrap else size - 1, 2)]
    return lax.ppermute(value, axis, pairs + [(j, i) for i, j in pairs])


def from_antipode(value):
    size = lax.axis_size("lon")
    return lax.ppermute(value, "lon", [(i, (i + size // 2) % size) for i in range(size)])


def body(thickness, wind_field):
    level_count, lon_count, lat_count = thickness.shape
    assert level_count == 1 and lon_count % ROWS == 0
    blocks = 2 * lat_count // RADIX
    kept = blocks // 2 + 1
    forward, inverse, twist, back, masks, rows = numpy_tables(lat_count)
    forward_tables = split_table(forward)
    inverse_tables = split_table(inverse)
    twist, back, masks, rows = [jnp.asarray(a) for a in (twist, back, masks, rows)]
    tables = (twist, back, masks, *forward_tables, *inverse_tables)
    f32 = jnp.float32
    array = lambda *shape: jax.ShapeDtypeStruct(shape, f32)
    scratch = lambda *shape: pltpu.VMEM(shape, f32)
    one, two = array(1, lon_count, lat_count), array(2, lon_count, lat_count)
    pack_shape = array(ROWS, lat_count + lat_count // ROWS)
    spectral = lambda count, width: (count * kept * lon_count, width * RADIX)
    working = lambda count: [
        scratch(count, lon_count, lat_count),
        scratch(count, lon_count, lat_count),
        scratch(*spectral(count, 2)),
        scratch(*spectral(count, 2)),
        scratch(*spectral(count, 4)),
    ]

    def call(kernel, name, outs, scratches, *args, in_specs=None, out_specs=None, cost=None):
        return pl.pallas_call(
            kernel,
            out_shape=outs,
            in_specs=in_specs or vmem(len(args)),
            out_specs=out_specs or vmem(len(outs)),
            scratch_shapes=scratches,
            compiler_params=params(),
            cost_estimate=cost
            and pl.CostEstimate(flops=cost, bytes_accessed=cost // 300, transcendentals=0),
            name=name,
        )(*args)

    winds = wind_field.reshape(2, lon_count, lat_count)
    far_first, far_second = from_antipode(winds), from_antipode(thickness)
    fields = jnp.concatenate([thickness, winds], 0)
    east, rest, height, near_pack, far_pack = call(
        gather_kernel, "gather_fields", [one, two, one, pack_shape, pack_shape], [], fields
    )
    for step in range(STEPS):
        final = step == STEPS - 1
        with_north = step == 0
        counts = (2, 1) if with_north else (1, 2)
        near = exchange(near_pack, "lon", 0)
        levels = [exchange(height, "lev", first) for first in (0, 1)]
        far = exchange(far_pack, "lon", 1)
        spectra = call(
            functools.partial(own_kernel, blocks, counts[0]),
            "own_spectra",
            [array(*spectral(count, 2)) for count in counts],
            [scratch(*spectral(3, 2))],
            near,
            east,
            rest,
            twist,
            masks,
            *forward_tables,
            in_specs=anywhere(1) + vmem(6),
        )
        east_next, zonal_terms, *north_terms = call(
            functools.partial(first_kernel, blocks, with_north),
            "eastward_wind",
            [one, two] + [two] * with_north,
            working(counts[0]),
            far_first,
            spectra[0],
            east,
            rest,
            near,
            far,
            rows,
            *tables,
            cost=FIRST_COST,
        )
        if not final:
            far_first = from_antipode(east_next)
        args = (far_second, spectra[1], rest, zonal_terms, *tables, *north_terms)
        kernel = functools.partial(second_kernel, blocks, with_north, final)
        if final:
            (rest_next,) = call(
                kernel, "north_and_height", [two], working(counts[1]), *args, cost=SECOND_COST
            )
            height, winds = call(
                last_kernel,
                "level_term",
                [one, two],
                [scratch(lon_count, lat_count), pltpu.SemaphoreType.DMA((2 + PIECES,))],
                east_next,
                rest_next,
                *levels,
                out_specs=anywhere(2),
            )
            return height, winds.reshape(wind_field.shape)
        rest, height, near_pack, far_pack = call(
            kernel,
            "north_and_height",
            [two, one, pack_shape, pack_shape],
            working(counts[1]),
            *args,
            east_next,
            *levels,
            cost=SECOND_COST,
        )
        east = east_next
        far_second = from_antipode(rest)


def solution(mesh):
    in_specs = (P("lev", "lon", None), P(None, "lev", "lon", None))
    out_specs = (P("lev", "lon", None), P(None, "lev", "lon", None))
    return jax.shard_map(body, mesh=mesh, in_specs=in_specs, out_specs=out_specs, check_vma=False)
```

```python
import functools
import math

import jax
import jax.numpy as jnp
import numpy as np
from jax import lax
from jax.experimental import pallas as pl
from jax.experimental.pallas import tpu as pltpu
from jax.sharding import PartitionSpec as P

STEPS = 2

courant = 0.2
mixing = 0.25
coriolis = 0.5
cos_floor = 0.25

RADIX = 128
ROWS = 8
FIRST_COST = 2_000_000_000
SECOND_COST = 2_000_000_000
EAST_COST = 2_000_000_000
REST_COST = 2_000_000_000
ZONAL_COST = 2000000000
LATE_ZONAL_COST = 1
PIECES = 4
HALO = 3


def split_table(table):
    high = table.astype(np.float32).astype(jnp.bfloat16)
    low = (table - high.astype(np.float64)).astype(np.float32).astype(jnp.bfloat16)
    return jnp.asarray(high), jnp.asarray(low)


@functools.lru_cache(maxsize=None)
def numpy_tables(lat_count):
    length = 2 * lat_count
    blocks = length // RADIX
    kept = blocks // 2 + 1
    centred = np.arange(RADIX) + 0.5
    order = np.arange(RADIX)
    signed = np.where(order < RADIX // 2, order, order - RADIX).astype(np.float64)
    angle = 2.0 * np.pi / RADIX * centred[:, None] * signed[None, :]
    cos, sin = np.cos(angle), np.sin(angle)
    forward = np.block([[cos, -sin], [sin, cos]])
    cos_t, sin_t = cos.T, sin.T
    weight = signed[:, None]
    inverse = np.block(
        [
            [cos_t, sin_t, -weight * sin_t, weight * cos_t],
            [-sin_t, cos_t, -weight * cos_t, -weight * sin_t],
        ]
    )
    first = np.arange(kept)
    turn = 2.0 * np.pi / length * first[:, None] * centred[None, :]
    twist = np.stack([np.cos(turn), -np.sin(turn)], 1)
    share = np.where((first == 0) | (first == blocks // 2), 1.0, 2.0)[:, None] / length
    back = np.stack([np.cos(turn) * share, np.sin(turn) * share], 1)
    slope_scale = 2.0 * np.pi * blocks / length
    back = np.concatenate([back, back * slope_scale], 1)
    wave = first[:, None] + blocks * signed[None, :]
    retained = (np.abs(wave) <= length // 3).astype(np.float64)
    plus = np.concatenate([retained, retained], 1)
    minus = np.concatenate([retained, -retained], 1)
    masks = np.stack([plus, minus, -minus], 1)
    latitude = (np.arange(lat_count) + 0.5) * (np.pi / lat_count) - 0.5 * np.pi
    rows = np.stack(
        [1.0 / np.maximum(np.cos(latitude), cos_floor), coriolis * np.sin(latitude)]
    )
    flat = lambda a: a.reshape(-1, a.shape[-1]).astype(np.float32)
    return forward, inverse, flat(twist), flat(back), flat(masks), rows.astype(np.float32)


def times(value, angle):
    real, imag = value
    cos, sin = math.cos(angle), math.sin(angle)
    quarter = round(angle / (math.pi / 2), 9)
    if quarter == int(quarter):
        turn = int(quarter) % 4
        return [(real, imag), (-imag, real), (-real, -imag), (imag, -real)][turn]
    if abs(abs(cos) - abs(sin)) < 1e-12:
        scale = abs(cos)
        a = real if cos > 0 else -real
        b = imag if cos > 0 else -imag
        c = imag if sin > 0 else -imag
        d = real if sin > 0 else -real
        return (scale * (a - c), scale * (b + d))
    return (real * cos - imag * sin, imag * cos + real * sin)


def add(a, b):
    return (a[0] + b[0], a[1] + b[1])


def sub(a, b):
    return (a[0] - b[0], a[1] - b[1])


def complex_dft(values, sign):
    n = len(values)
    if n == 1:
        return values
    half = n // 2
    even = complex_dft([add(values[m], values[m + half]) for m in range(half)], sign)
    odd = complex_dft(
        [
            times(sub(values[m], values[m + half]), sign * 2 * math.pi * m / n)
            for m in range(half)
        ],
        sign,
    )
    return [even[q // 2] if q % 2 == 0 else odd[q // 2] for q in range(n)]


def odd_outputs(values):
    r = len(values)
    if r == 1:
        return {1: (values[0], None)}
    half = r // 2
    turned = [
        times((values[m], -values[m + half]), -math.pi * m / r) for m in range(half)
    ]
    out = {}
    for q, value in enumerate(complex_dft(turned, -1)):
        j = 4 * q + 1
        out[j if j <= r else 2 * r - j] = value if j <= r else (value[0], -value[1])
    return out


def half_circle_forward(values):
    n = len(values)
    out = {j: value for j, value in odd_outputs(values).items()}
    scale = 2
    while len(values) > 1:
        half = len(values) // 2
        difference = [values[m] - values[m + half] for m in range(half)]
        values = [values[m] + values[m + half] for m in range(half)]
        for j, value in odd_outputs(difference).items():
            out[j * scale] = value
        scale *= 2
    out[0] = (values[0], None)
    return [out[k] for k in range(n + 1)]


def odd_inputs(values, r):
    if r == 1:
        return [values[1][0]]
    half = r // 2
    gathered = []
    for q in range(half):
        j = 4 * q + 1
        if j <= r:
            gathered.append(values[j])
        else:
            real, imag = values[2 * r - j]
            gathered.append((real, -imag))
    turned = [
        times(value, math.pi * m / r) for m, value in enumerate(complex_dft(gathered, 1))
    ]
    return [value[0] for value in turned] + [-value[1] for value in turned]


def half_circle_inverse(values):
    n = len(values) - 1
    result = [values[0][0]]
    size = 1
    while size < n:
        step = n // size
        difference = odd_inputs({j: values[j * step] for j in range(1, size + 1, 2)}, size)
        result = [result[m] + difference[m] for m in range(size)] + [
            result[m] - difference[m] for m in range(size)
        ]
        size *= 2
    last = odd_inputs({j: values[j] for j in range(1, n + 1, 2)}, n)
    return [result[m] + last[m] for m in range(n)]


def tile(index):
    return pl.ds(index * RADIX, RADIX)


def split(value):
    high = value.astype(jnp.bfloat16)
    return high, (value - high.astype(jnp.float32)).astype(jnp.bfloat16)


def triple_product(value, high_table, low_table):
    high, low = split(value)
    left = jnp.concatenate([high, low, high], 1)
    right = jnp.concatenate([high_table, high_table, low_table], 0)
    return jnp.dot(left, right, preferred_element_type=jnp.float32)


def forward_stage(slabs_of, groups, twist, turned, blocks):
    for group in range(groups):
        slabs = slabs_of(group)
        for k, (real, imag) in enumerate(half_circle_forward(slabs)):
            at = pl.ds((k * groups + group) * ROWS, ROWS)
            cos, sin = twist[2 * k : 2 * k + 1, :], twist[2 * k + 1 : 2 * k + 2, :]
            if imag is None:
                turned[at, tile(0)] = real * cos
                turned[at, tile(1)] = real * sin
            else:
                turned[at, tile(0)] = real * cos - imag * sin
                turned[at, tile(1)] = real * sin + imag * cos


def row_groups(lon_count):
    return [slice(i, i + ROWS) for i in range(0, lon_count, ROWS)]


def pack_rows(pack, lat_count, field, index, rows):
    if field < 2:
        pack[HALO * field : HALO * field + HALO, tile(index)] = rows
    else:
        pack[2 * HALO : ROWS, tile(index)] = rows[: ROWS - 2 * HALO]
        pack[index // 2 : index // 2 + 1, pl.ds(lat_count + index % 2 * RADIX, RADIX)] = rows[
            ROWS - 2 * HALO :
        ]


def halo_rows(pack, lat_count, field, index):
    if field < 2:
        return pack[HALO * field : HALO * field + HALO, tile(index)]
    last = pack[index // 2 : index // 2 + 1, pl.ds(lat_count + index % 2 * RADIX, RADIX)]
    return jnp.concatenate([pack[2 * HALO : ROWS, tile(index)], last], 0)


def field_at(east, rest, field, *at):
    return east[(0, *at)] if field == 0 else rest[(field - 1, *at)]


def odd_device():
    return lax.rem(lax.axis_index("lon"), 2) == 1


def pack_tile(field, index, rows, near_pack, far_pack, lat_count):
    first, last = rows[:HALO], rows[rows.shape[0] - HALO :]
    odd = odd_device()
    pack_rows(near_pack, lat_count, field, index, jnp.where(odd, first, last))
    pack_rows(far_pack, lat_count, field, index, jnp.where(odd, last, first))


def gather_kernel(fields, east, rest, near_pack, far_pack):
    lat_count = fields.shape[-1]
    for index in range(lat_count // RADIX):
        at = tile(index)
        thickness, eastward, northward = [fields[i, :, at] for i in range(3)]
        east[0, :, at] = eastward
        rest[0, :, at] = northward
        rest[1, :, at] = thickness
        for field, rows in enumerate((eastward, northward, thickness)):
            pack_tile(field, index, rows, near_pack, far_pack, lat_count)


def own_kernel(blocks, split_at, near, east, rest, twist, masks, high, low, *refs):
    first, second, turned = refs[-3:]
    kept = blocks // 2 + 1
    lon_count = east.shape[1]
    groups = [(field, at) for field in range(3) for at in row_groups(lon_count)]

    def slabs_of(group):
        field, at = groups[group]
        return [field_at(east, rest, field, at, tile(m)) for m in range(blocks // 2)]

    forward_stage(slabs_of, len(groups), twist, turned, blocks)
    result = triple_product(turned[...], high[...], low[...])
    cut, span = split_at * lon_count, 3 * lon_count
    for k in range(kept):
        value = result[k * span : k * span + span, :] * masks[3 * k : 3 * k + 1, :]
        first[k * cut : k * cut + cut, :] = value[:cut]
        second[k * (span - cut) : (k + 1) * (span - cut), :] = value[cut:]


def transform(blocks, parities, far, spectrum, tables, smooth, slope, work):
    twist, back, masks, forward_high, forward_low, inverse_high, inverse_low = tables
    turned, weighted, spread = work
    kept = blocks // 2 + 1
    count, lon_count = far.shape[:2]
    length = blocks * RADIX
    groups = [(field, at) for field in range(count) for at in row_groups(lon_count)]

    def slabs_of(group):
        field, at = groups[group]
        return [far[field, at, tile(m)] for m in range(blocks // 2)]

    forward_stage(slabs_of, len(groups), twist, turned, blocks)
    result = triple_product(turned[...], forward_high[...], forward_low[...])
    for k in range(kept):
        for field, parity in enumerate(parities):
            at = (k * count + field) * lon_count
            row = 3 * k + (1 if parity > 0 else 2)
            weighted[at : at + lon_count, :] = (
                spectrum[at : at + lon_count, :]
                + result[at : at + lon_count, :] * masks[row : row + 1, :]
            )
    spread[...] = triple_product(weighted[...], inverse_high[...], inverse_low[...])
    for group, (field, out) in enumerate(groups):
        smooth_terms, slope_terms = [], []
        for k in range(kept):
            at = pl.ds((k * len(groups) + group) * ROWS, ROWS)
            real, imag, slope_real, slope_imag = [spread[at, tile(i)] for i in range(4)]
            cos, sin, slope_cos, slope_sin = [back[4 * k + i : 4 * k + i + 1, :] for i in range(4)]
            turn_real = real * cos - imag * sin
            turn_imag = real * sin + imag * cos
            wave = 2.0 * math.pi * k / length
            smooth_terms.append((turn_real, turn_imag))
            slope_terms.append(
                (
                    slope_real * slope_cos - slope_imag * slope_sin - wave * turn_imag,
                    slope_real * slope_sin + slope_imag * slope_cos + wave * turn_real,
                )
            )
        for m, value in enumerate(half_circle_inverse(smooth_terms)):
            smooth[field, out, tile(m)] = value
        for m, value in enumerate(half_circle_inverse(slope_terms)):
            slope[field, out, tile(m)] = value


def zonal_parts(index, east, rest, near, far, rows):
    lon_count, lat_count = east.shape[1:]
    odd = odd_device()
    here = [field_at(east, rest, field, slice(None), tile(index)) for field in range(3)]
    secant, turning = rows[0:1, tile(index)], rows[1:2, tile(index)]
    zonal = []
    for field in range(3):
        close = halo_rows(near, lat_count, field, index)
        away = halo_rows(far, lat_count, field, index)
        line = jnp.concatenate(
            [jnp.where(odd, close, away), here[field], jnp.where(odd, away, close)], 0
        )
        at = [line[i : i + lon_count] for i in range(2 * HALO + 1)]
        difference = (
            (45.0 / 60.0) * (at[4] - at[2])
            - (9.0 / 60.0) * (at[5] - at[1])
            + (1.0 / 60.0) * (at[6] - at[0])
        )
        zonal.append(secant * difference)
    eastward, northward, thick = here
    return here, (
        turning * northward - eastward * zonal[0] - zonal[2],
        -eastward * zonal[1] - turning * eastward,
        -eastward * zonal[2] - thick * zonal[0],
    )


def first_kernel(blocks, far_rows, spectrum, east, rest, zonal_terms, *refs):
    tables, refs = refs[:7], refs[7:]
    east_next, north_terms, smooth, slope, *work = refs
    transform(blocks, (-1, -1), far_rows, spectrum, tables, smooth, slope, work)
    north_terms[0] = smooth[1]
    north_terms[1] = slope[1]
    for index in range(east.shape[-1] // RADIX):
        at = tile(index)
        tendency = zonal_terms[0, :, at] - rest[0, :, at] * slope[0, :, at]
        east_next[0, :, at] = smooth[0, :, at] + courant * tendency


def second_kernel(
    blocks, far_rows, spectrum, rest, zonal_terms, north_terms, east_next, levels, others, *refs
):
    tables, refs = refs[:7], refs[7:]
    rest_next, height_next, near_pack, far_pack, smooth, slope, *work = refs
    lat_count = rest.shape[-1]
    transform(blocks, (1,), far_rows, spectrum, tables, smooth, slope, work)
    for index in range(lat_count // RADIX):
        at = tile(index)
        northward, thick = rest[0, :, at], rest[1, :, at]
        north_slope, thick_slope = north_terms[1, :, at], slope[0, :, at]
        vertical = levels[0, :, at] + others[0, :, at] - 2.0 * thick
        north_tendency = zonal_terms[1, :, at] - northward * north_slope - thick_slope
        thick_tendency = (
            zonal_terms[2, :, at]
            - northward * thick_slope
            - thick * north_slope
            + mixing * vertical
        )
        values = (
            north_terms[0, :, at] + courant * north_tendency,
            smooth[0, :, at] + courant * thick_tendency,
        )
        for field in range(2):
            rest_next[field, :, at] = values[field]
        height_next[0, :, at] = values[1]
        for field, moved in enumerate((east_next[0, :, at], *values)):
            pack_tile(field, index, moved, near_pack, far_pack, lat_count)


def transform_kernel(blocks, parities, far_rows, spectrum, *refs):
    tables, (smooth, slope, *work) = refs[:7], refs[7:]
    transform(blocks, parities, far_rows, spectrum, tables, smooth, slope, work)


def zonal_kernel(east, rest, near, far, rows, out):
    for index in range(east.shape[-1] // RADIX):
        _, terms = zonal_parts(index, east, rest, near, far, rows)
        for field in range(3):
            out[field, :, tile(index)] = terms[field]


def last_kernel(
    rest,
    zonal_terms,
    east_smooth,
    east_slope,
    rest_smooth,
    rest_slope,
    levels,
    others,
    height_out,
    wind_out,
    staged,
    sems,
):
    tiles = rest.shape[-1] // RADIX
    copies = []
    for piece in range(PIECES):
        for index in range(piece * tiles // PIECES, (piece + 1) * tiles // PIECES):
            at = tile(index)
            northward, thick = rest[0, :, at], rest[1, :, at]
            north_slope, thick_slope = rest_slope[0, :, at], rest_slope[1, :, at]
            vertical = levels[0, :, at] + others[0, :, at] - 2.0 * thick
            tendencies = (
                zonal_terms[0, :, at] - northward * east_slope[0, :, at],
                zonal_terms[1, :, at] - northward * north_slope - thick_slope,
                zonal_terms[2, :, at]
                - northward * thick_slope
                - thick * north_slope
                + mixing * vertical,
            )
            smooths = (east_smooth[0, :, at], rest_smooth[0, :, at], rest_smooth[1, :, at])
            for field in range(3):
                staged[field, :, at] = smooths[field] + courant * tendencies[field]
        span = pl.ds(piece * tiles // PIECES * RADIX, tiles // PIECES * RADIX)
        targets = (wind_out.at[0, :, span], wind_out.at[1, :, span], height_out.at[0, :, span])
        for field, target in enumerate(targets):
            copies.append(
                pltpu.make_async_copy(
                    staged.at[field, :, span], target, sems.at[3 * piece + field]
                )
            )
            copies[-1].start()
    for copy in copies:
        copy.wait()


def vmem(count):
    return [pl.BlockSpec(memory_space=pltpu.VMEM)] * count


def anywhere(count):
    return [pl.BlockSpec(memory_space=pl.ANY)] * count


def params():
    return pltpu.CompilerParams(vmem_limit_bytes=24 * 1024 * 1024)


def exchange(value, axis, first):
    size = lax.axis_size(axis)
    wrap = axis == "lon"
    pairs = [(i, (i + 1) % size) for i in range(first, size if wrap else size - 1, 2)]
    return lax.ppermute(value, axis, pairs + [(j, i) for i, j in pairs])


def from_antipode(value):
    size = lax.axis_size("lon")
    return lax.ppermute(value, "lon", [(i, (i + size // 2) % size) for i in range(size)])


def body(thickness, wind_field):
    level_count, lon_count, lat_count = thickness.shape
    assert level_count == 1 and lon_count % ROWS == 0
    blocks = 2 * lat_count // RADIX
    kept = blocks // 2 + 1
    forward, inverse, twist, back, masks, rows = numpy_tables(lat_count)
    forward_tables = split_table(forward)
    inverse_tables = split_table(inverse)
    twist, back, masks, rows = [jnp.asarray(a) for a in (twist, back, masks, rows)]
    tables = (twist, back, masks, *forward_tables, *inverse_tables)
    f32 = jnp.float32
    array = lambda *shape: jax.ShapeDtypeStruct(shape, f32)
    scratch = lambda *shape: pltpu.VMEM(shape, f32)
    one, two = array(1, lon_count, lat_count), array(2, lon_count, lat_count)
    pack_shape = array(ROWS, lat_count + lat_count // ROWS)
    spectral = lambda count, width: (count * kept * lon_count, width * RADIX)
    working = lambda count: [
        scratch(count, lon_count, lat_count),
        scratch(count, lon_count, lat_count),
        scratch(*spectral(count, 2)),
        scratch(*spectral(count, 2)),
        scratch(*spectral(count, 4)),
    ]

    def call(kernel, name, outs, scratches, *args, in_specs=None, out_specs=None, cost=None):
        return pl.pallas_call(
            kernel,
            out_shape=outs,
            in_specs=in_specs or vmem(len(args)),
            out_specs=out_specs or vmem(len(outs)),
            scratch_shapes=scratches,
            compiler_params=params(),
            cost_estimate=cost
            and pl.CostEstimate(flops=cost, bytes_accessed=cost // 300, transcendentals=0),
            name=name,
        )(*args)

    winds = wind_field.reshape(2, lon_count, lat_count)
    far_first, far_second = from_antipode(winds), from_antipode(thickness)
    fields = jnp.concatenate([thickness, winds], 0)
    east, rest, near_pack, far_pack = call(
        gather_kernel, "gather_fields", [one, two, pack_shape, pack_shape], [], fields
    )
    height = thickness
    for step in range(STEPS):
        final = step == STEPS - 1
        counts = (2, 1) if step == 0 else (1, 2)
        near = exchange(near_pack, "lon", 0)
        levels = [exchange(height, "lev", first) for first in (0, 1)]
        far = exchange(far_pack, "lon", 1)
        spectra = call(
            functools.partial(own_kernel, blocks, counts[0]),
            "own_spectra",
            [array(*spectral(count, 2)) for count in counts],
            [scratch(*spectral(3, 2))],
            near,
            east,
            rest,
            twist,
            masks,
            *forward_tables,
            *inverse_tables,
            back,
            in_specs=anywhere(1) + vmem(9),
        )
        (zonal_terms,) = call(
            zonal_kernel,
            "zonal_terms",
            [array(3, lon_count, lat_count)],
            [],
            east,
            rest,
            near,
            far,
            rows,
            cost=LATE_ZONAL_COST if final else ZONAL_COST,
        )
        if final:
            break
        east_next, north_terms = call(
            functools.partial(first_kernel, blocks),
            "eastward_wind",
            [one, two],
            working(2),
            far_first,
            spectra[0],
            east,
            rest,
            zonal_terms,
            *tables,
            cost=FIRST_COST,
        )
        far_first = from_antipode(east_next)
        rest, height, near_pack, far_pack = call(
            functools.partial(second_kernel, blocks),
            "north_and_height",
            [two, one, pack_shape, pack_shape],
            working(1),
            far_second,
            spectra[1],
            rest,
            zonal_terms,
            north_terms,
            east_next,
            *levels,
            *tables,
            cost=SECOND_COST,
        )
        east = east_next
        far_second = from_antipode(rest)

    east_terms = call(
        functools.partial(transform_kernel, blocks, (-1,)),
        "transform_east",
        [one, one],
        working(1)[2:],
        far_first,
        spectra[0],
        *tables,
        cost=EAST_COST,
    )
    rest_terms = call(
        functools.partial(transform_kernel, blocks, (-1, 1)),
        "transform_rest",
        [two, two],
        working(2)[2:],
        far_second,
        spectra[1],
        *tables,
        cost=REST_COST,
    )
    height, winds = call(
        last_kernel,
        "last_update",
        [one, two],
        [scratch(3, lon_count, lat_count), pltpu.SemaphoreType.DMA((3 * PIECES,))],
        rest,
        zonal_terms,
        *east_terms,
        *rest_terms,
        *levels,
        out_specs=anywhere(2),
    )
    return height, winds.reshape(wind_field.shape)


def solution(mesh):
    in_specs = (P("lev", "lon", None), P(None, "lev", "lon", None))
    out_specs = (P("lev", "lon", None), P(None, "lev", "lon", None))
    return jax.shard_map(body, mesh=mesh, in_specs=in_specs, out_specs=out_specs, check_vma=False)
```

```python
import functools
import math

import jax
import jax.numpy as jnp
import numpy as np
from jax import lax
from jax.experimental import pallas as pl
from jax.experimental.pallas import tpu as pltpu
from jax.sharding import PartitionSpec as P

STEPS = 2

courant = 0.2
mixing = 0.25
coriolis = 0.5
cos_floor = 0.25

RADIX = 128
ROWS = 8
FIRST_COST = 2_000_000_000
SECOND_COST = 2_000_000_000
EAST_COST = 2_000_000_000
REST_COST = 2_000_000_000
ZONAL_COST = 2000000000
LATE_ZONAL_COST = 1
PIECES = 4
HALO = 3


def split_table(table):
    high = table.astype(np.float32).astype(jnp.bfloat16)
    low = (table - high.astype(np.float64)).astype(np.float32).astype(jnp.bfloat16)
    return jnp.asarray(high), jnp.asarray(low)


@functools.lru_cache(maxsize=None)
def numpy_tables(lat_count):
    length = 2 * lat_count
    blocks = length // RADIX
    kept = blocks // 2 + 1
    centred = np.arange(RADIX) + 0.5
    order = np.arange(RADIX)
    signed = np.where(order < RADIX // 2, order, order - RADIX).astype(np.float64)
    angle = 2.0 * np.pi / RADIX * centred[:, None] * signed[None, :]
    cos, sin = np.cos(angle), np.sin(angle)
    forward = np.block([[cos, -sin], [sin, cos]])
    cos_t, sin_t = cos.T, sin.T
    weight = signed[:, None]
    inverse = np.block(
        [
            [cos_t, sin_t, -weight * sin_t, weight * cos_t],
            [-sin_t, cos_t, -weight * cos_t, -weight * sin_t],
        ]
    )
    first = np.arange(kept)
    turn = 2.0 * np.pi / length * first[:, None] * centred[None, :]
    twist = np.stack([np.cos(turn), -np.sin(turn)], 1)
    share = np.where((first == 0) | (first == blocks // 2), 1.0, 2.0)[:, None] / length
    back = np.stack([np.cos(turn) * share, np.sin(turn) * share], 1)
    slope_scale = 2.0 * np.pi * blocks / length
    back = np.concatenate([back, back * slope_scale], 1)
    wave = first[:, None] + blocks * signed[None, :]
    retained = (np.abs(wave) <= length // 3).astype(np.float64)
    plus = np.concatenate([retained, retained], 1)
    minus = np.concatenate([retained, -retained], 1)
    masks = np.stack([plus, minus, -minus], 1)
    latitude = (np.arange(lat_count) + 0.5) * (np.pi / lat_count) - 0.5 * np.pi
    rows = np.stack(
        [1.0 / np.maximum(np.cos(latitude), cos_floor), coriolis * np.sin(latitude)]
    )
    flat = lambda a: a.reshape(-1, a.shape[-1]).astype(np.float32)
    return forward, inverse, flat(twist), flat(back), flat(masks), rows.astype(np.float32)


def times(value, angle):
    real, imag = value
    cos, sin = math.cos(angle), math.sin(angle)
    quarter = round(angle / (math.pi / 2), 9)
    if quarter == int(quarter):
        turn = int(quarter) % 4
        return [(real, imag), (-imag, real), (-real, -imag), (imag, -real)][turn]
    if abs(abs(cos) - abs(sin)) < 1e-12:
        scale = abs(cos)
        a = real if cos > 0 else -real
        b = imag if cos > 0 else -imag
        c = imag if sin > 0 else -imag
        d = real if sin > 0 else -real
        return (scale * (a - c), scale * (b + d))
    return (real * cos - imag * sin, imag * cos + real * sin)


def add(a, b):
    return (a[0] + b[0], a[1] + b[1])


def sub(a, b):
    return (a[0] - b[0], a[1] - b[1])


def complex_dft(values, sign):
    n = len(values)
    if n == 1:
        return values
    half = n // 2
    even = complex_dft([add(values[m], values[m + half]) for m in range(half)], sign)
    odd = complex_dft(
        [
            times(sub(values[m], values[m + half]), sign * 2 * math.pi * m / n)
            for m in range(half)
        ],
        sign,
    )
    return [even[q // 2] if q % 2 == 0 else odd[q // 2] for q in range(n)]


def odd_outputs(values):
    r = len(values)
    if r == 1:
        return {1: (values[0], None)}
    half = r // 2
    turned = [
        times((values[m], -values[m + half]), -math.pi * m / r) for m in range(half)
    ]
    out = {}
    for q, value in enumerate(complex_dft(turned, -1)):
        j = 4 * q + 1
        out[j if j <= r else 2 * r - j] = value if j <= r else (value[0], -value[1])
    return out


def half_circle_forward(values):
    n = len(values)
    out = {j: value for j, value in odd_outputs(values).items()}
    scale = 2
    while len(values) > 1:
        half = len(values) // 2
        difference = [values[m] - values[m + half] for m in range(half)]
        values = [values[m] + values[m + half] for m in range(half)]
        for j, value in odd_outputs(difference).items():
            out[j * scale] = value
        scale *= 2
    out[0] = (values[0], None)
    return [out[k] for k in range(n + 1)]


def odd_inputs(values, r):
    if r == 1:
        return [values[1][0]]
    half = r // 2
    gathered = []
    for q in range(half):
        j = 4 * q + 1
        if j <= r:
            gathered.append(values[j])
        else:
            real, imag = values[2 * r - j]
            gathered.append((real, -imag))
    turned = [
        times(value, math.pi * m / r) for m, value in enumerate(complex_dft(gathered, 1))
    ]
    return [value[0] for value in turned] + [-value[1] for value in turned]


def half_circle_inverse(values):
    n = len(values) - 1
    result = [values[0][0]]
    size = 1
    while size < n:
        step = n // size
        difference = odd_inputs({j: values[j * step] for j in range(1, size + 1, 2)}, size)
        result = [result[m] + difference[m] for m in range(size)] + [
            result[m] - difference[m] for m in range(size)
        ]
        size *= 2
    last = odd_inputs({j: values[j] for j in range(1, n + 1, 2)}, n)
    return [result[m] + last[m] for m in range(n)]


def tile(index):
    return pl.ds(index * RADIX, RADIX)


def split(value):
    high = value.astype(jnp.bfloat16)
    return high, (value - high.astype(jnp.float32)).astype(jnp.bfloat16)


def triple_product(value, high_table, low_table):
    high, low = split(value)
    left = jnp.concatenate([high, low, high], 1)
    right = jnp.concatenate([high_table, high_table, low_table], 0)
    return jnp.dot(left, right, preferred_element_type=jnp.float32)


def forward_stage(slabs_of, groups, twist, turned, blocks):
    for group in range(groups):
        slabs = slabs_of(group)
        for k, (real, imag) in enumerate(half_circle_forward(slabs)):
            at = pl.ds((k * groups + group) * ROWS, ROWS)
            cos, sin = twist[2 * k : 2 * k + 1, :], twist[2 * k + 1 : 2 * k + 2, :]
            if imag is None:
                turned[at, tile(0)] = real * cos
                turned[at, tile(1)] = real * sin
            else:
                turned[at, tile(0)] = real * cos - imag * sin
                turned[at, tile(1)] = real * sin + imag * cos


def row_groups(lon_count):
    return [slice(i, i + ROWS) for i in range(0, lon_count, ROWS)]


def pack_rows(pack, lat_count, field, index, rows):
    if field < 2:
        pack[HALO * field : HALO * field + HALO, tile(index)] = rows
    else:
        pack[2 * HALO : ROWS, tile(index)] = rows[: ROWS - 2 * HALO]
        pack[index // 2 : index // 2 + 1, pl.ds(lat_count + index % 2 * RADIX, RADIX)] = rows[
            ROWS - 2 * HALO :
        ]


def halo_rows(pack, lat_count, field, index):
    if field < 2:
        return pack[HALO * field : HALO * field + HALO, tile(index)]
    last = pack[index // 2 : index // 2 + 1, pl.ds(lat_count + index % 2 * RADIX, RADIX)]
    return jnp.concatenate([pack[2 * HALO : ROWS, tile(index)], last], 0)


def field_at(east, rest, field, *at):
    return east[(0, *at)] if field == 0 else rest[(field - 1, *at)]


def odd_device():
    return lax.rem(lax.axis_index("lon"), 2) == 1


def pack_tile(field, index, rows, near_pack, far_pack, lat_count):
    first, last = rows[:HALO], rows[rows.shape[0] - HALO :]
    odd = odd_device()
    pack_rows(near_pack, lat_count, field, index, jnp.where(odd, first, last))
    pack_rows(far_pack, lat_count, field, index, jnp.where(odd, last, first))


def gather_kernel(fields, east, rest, near_pack, far_pack):
    lat_count = fields.shape[-1]
    for index in range(lat_count // RADIX):
        at = tile(index)
        thickness, eastward, northward = [fields[i, :, at] for i in range(3)]
        east[0, :, at] = eastward
        rest[0, :, at] = northward
        rest[1, :, at] = thickness
        for field, rows in enumerate((eastward, northward, thickness)):
            pack_tile(field, index, rows, near_pack, far_pack, lat_count)


def own_kernel(blocks, split_at, near, east, rest, twist, masks, high, low, *refs):
    first, second, turned = refs[-3:]
    kept = blocks // 2 + 1
    lon_count = east.shape[1]
    groups = [(field, at) for field in range(3) for at in row_groups(lon_count)]

    def slabs_of(group):
        field, at = groups[group]
        return [field_at(east, rest, field, at, tile(m)) for m in range(blocks // 2)]

    forward_stage(slabs_of, len(groups), twist, turned, blocks)
    result = triple_product(turned[...], high[...], low[...])
    cut, span = split_at * lon_count, 3 * lon_count
    for k in range(kept):
        value = result[k * span : k * span + span, :] * masks[3 * k : 3 * k + 1, :]
        first[k * cut : k * cut + cut, :] = value[:cut]
        second[k * (span - cut) : (k + 1) * (span - cut), :] = value[cut:]


def transform(blocks, parities, far, spectrum, tables, smooth, slope, work):
    twist, back, masks, forward_high, forward_low, inverse_high, inverse_low = tables
    turned, weighted, spread = work
    kept = blocks // 2 + 1
    count, lon_count = far.shape[:2]
    length = blocks * RADIX
    groups = [(field, at) for field in range(count) for at in row_groups(lon_count)]

    def slabs_of(group):
        field, at = groups[group]
        return [far[field, at, tile(m)] for m in range(blocks // 2)]

    forward_stage(slabs_of, len(groups), twist, turned, blocks)
    result = triple_product(turned[...], forward_high[...], forward_low[...])
    for k in range(kept):
        for field, parity in enumerate(parities):
            at = (k * count + field) * lon_count
            row = 3 * k + (1 if parity > 0 else 2)
            weighted[at : at + lon_count, :] = (
                spectrum[at : at + lon_count, :]
                + result[at : at + lon_count, :] * masks[row : row + 1, :]
            )
    spread[...] = triple_product(weighted[...], inverse_high[...], inverse_low[...])
    for group, (field, out) in enumerate(groups):
        smooth_terms, slope_terms = [], []
        for k in range(kept):
            at = pl.ds((k * len(groups) + group) * ROWS, ROWS)
            real, imag, slope_real, slope_imag = [spread[at, tile(i)] for i in range(4)]
            cos, sin, slope_cos, slope_sin = [back[4 * k + i : 4 * k + i + 1, :] for i in range(4)]
            turn_real = real * cos - imag * sin
            turn_imag = real * sin + imag * cos
            wave = 2.0 * math.pi * k / length
            smooth_terms.append((turn_real, turn_imag))
            slope_terms.append(
                (
                    slope_real * slope_cos - slope_imag * slope_sin - wave * turn_imag,
                    slope_real * slope_sin + slope_imag * slope_cos + wave * turn_real,
                )
            )
        for m, value in enumerate(half_circle_inverse(smooth_terms)):
            smooth[field, out, tile(m)] = value
        for m, value in enumerate(half_circle_inverse(slope_terms)):
            slope[field, out, tile(m)] = value


def zonal_parts(index, east, rest, near, far, rows):
    lon_count, lat_count = east.shape[1:]
    odd = odd_device()
    here = [field_at(east, rest, field, slice(None), tile(index)) for field in range(3)]
    secant, turning = rows[0:1, tile(index)], rows[1:2, tile(index)]
    zonal = []
    for field in range(3):
        close = halo_rows(near, lat_count, field, index)
        away = halo_rows(far, lat_count, field, index)
        line = jnp.concatenate(
            [jnp.where(odd, close, away), here[field], jnp.where(odd, away, close)], 0
        )
        at = [line[i : i + lon_count] for i in range(2 * HALO + 1)]
        difference = (
            (45.0 / 60.0) * (at[4] - at[2])
            - (9.0 / 60.0) * (at[5] - at[1])
            + (1.0 / 60.0) * (at[6] - at[0])
        )
        zonal.append(secant * difference)
    eastward, northward, thick = here
    return here, (
        turning * northward - eastward * zonal[0] - zonal[2],
        -eastward * zonal[1] - turning * eastward,
        -eastward * zonal[2] - thick * zonal[0],
    )


def first_kernel(blocks, far_rows, spectrum, east, rest, zonal_terms, *refs):
    tables, refs = refs[:7], refs[7:]
    east_next, north_terms, smooth, slope, *work = refs
    transform(blocks, (-1, -1), far_rows, spectrum, tables, smooth, slope, work)
    north_terms[0] = smooth[1]
    north_terms[1] = slope[1]
    for index in range(east.shape[-1] // RADIX):
        at = tile(index)
        tendency = zonal_terms[0, :, at] - rest[0, :, at] * slope[0, :, at]
        east_next[0, :, at] = smooth[0, :, at] + courant * tendency


def second_kernel(
    blocks, far_rows, spectrum, rest, zonal_terms, north_terms, east_next, levels, others, *refs
):
    tables, refs = refs[:7], refs[7:]
    rest_next, height_next, near_pack, far_pack, smooth, slope, *work = refs
    lat_count = rest.shape[-1]
    transform(blocks, (1,), far_rows, spectrum, tables, smooth, slope, work)
    for index in range(lat_count // RADIX):
        at = tile(index)
        northward, thick = rest[0, :, at], rest[1, :, at]
        north_slope, thick_slope = north_terms[1, :, at], slope[0, :, at]
        vertical = levels[0, :, at] + others[0, :, at] - 2.0 * thick
        north_tendency = zonal_terms[1, :, at] - northward * north_slope - thick_slope
        thick_tendency = (
            zonal_terms[2, :, at]
            - northward * thick_slope
            - thick * north_slope
            + mixing * vertical
        )
        values = (
            north_terms[0, :, at] + courant * north_tendency,
            smooth[0, :, at] + courant * thick_tendency,
        )
        for field in range(2):
            rest_next[field, :, at] = values[field]
        height_next[0, :, at] = values[1]
        for field, moved in enumerate((east_next[0, :, at], *values)):
            pack_tile(field, index, moved, near_pack, far_pack, lat_count)


def transform_kernel(blocks, parities, far_rows, spectrum, *refs):
    tables, (smooth, slope, *work) = refs[:7], refs[7:]
    transform(blocks, parities, far_rows, spectrum, tables, smooth, slope, work)


def zonal_kernel(east, rest, near, far, rows, out):
    for index in range(east.shape[-1] // RADIX):
        _, terms = zonal_parts(index, east, rest, near, far, rows)
        for field in range(3):
            out[field, :, tile(index)] = terms[field]


def rest_kernel(
    blocks, far_rows, spectrum, rest, zonal_terms, east_smooth, east_slope, *refs
):
    tables, (out, smooth, slope, *work) = refs[:7], refs[7:]
    transform(blocks, (-1, 1), far_rows, spectrum, tables, smooth, slope, work)
    for index in range(rest.shape[-1] // RADIX):
        at = tile(index)
        northward, thick = rest[0, :, at], rest[1, :, at]
        north_slope, thick_slope = slope[0, :, at], slope[1, :, at]
        tendencies = (
            zonal_terms[0, :, at] - northward * east_slope[0, :, at],
            zonal_terms[1, :, at] - northward * north_slope - thick_slope,
            zonal_terms[2, :, at]
            - northward * thick_slope
            - thick * north_slope
            - 2.0 * mixing * thick,
        )
        smooths = (east_smooth[0, :, at], smooth[0, :, at], smooth[1, :, at])
        for field in range(3):
            out[field, :, at] = smooths[field] + courant * tendencies[field]


def last_kernel(fields, levels, others, height_out, wind_out, height, sems):
    copies = [
        pltpu.make_async_copy(fields.at[0], wind_out.at[0], sems.at[0]),
        pltpu.make_async_copy(fields.at[1], wind_out.at[1], sems.at[1]),
        pltpu.make_async_copy(height, height_out.at[0], sems.at[2]),
    ]
    copies[0].start()
    copies[1].start()
    for index in range(height.shape[-1] // RADIX):
        at = tile(index)
        neighbours = levels[0, :, at] + others[0, :, at]
        height[:, at] = fields[2, :, at] + (courant * mixing) * neighbours
    copies[2].start()
    for copy in copies:
        copy.wait()


def vmem(count):
    return [pl.BlockSpec(memory_space=pltpu.VMEM)] * count


def anywhere(count):
    return [pl.BlockSpec(memory_space=pl.ANY)] * count


def params():
    return pltpu.CompilerParams(vmem_limit_bytes=24 * 1024 * 1024)


def exchange(value, axis, first):
    size = lax.axis_size(axis)
    wrap = axis == "lon"
    pairs = [(i, (i + 1) % size) for i in range(first, size if wrap else size - 1, 2)]
    return lax.ppermute(value, axis, pairs + [(j, i) for i, j in pairs])


def from_antipode(value):
    size = lax.axis_size("lon")
    return lax.ppermute(value, "lon", [(i, (i + size // 2) % size) for i in range(size)])


def body(thickness, wind_field):
    level_count, lon_count, lat_count = thickness.shape
    assert level_count == 1 and lon_count % ROWS == 0
    blocks = 2 * lat_count // RADIX
    kept = blocks // 2 + 1
    forward, inverse, twist, back, masks, rows = numpy_tables(lat_count)
    forward_tables = split_table(forward)
    inverse_tables = split_table(inverse)
    twist, back, masks, rows = [jnp.asarray(a) for a in (twist, back, masks, rows)]
    tables = (twist, back, masks, *forward_tables, *inverse_tables)
    f32 = jnp.float32
    array = lambda *shape: jax.ShapeDtypeStruct(shape, f32)
    scratch = lambda *shape: pltpu.VMEM(shape, f32)
    one, two = array(1, lon_count, lat_count), array(2, lon_count, lat_count)
    pack_shape = array(ROWS, lat_count + lat_count // ROWS)
    spectral = lambda count, width: (count * kept * lon_count, width * RADIX)
    working = lambda count: [
        scratch(count, lon_count, lat_count),
        scratch(count, lon_count, lat_count),
        scratch(*spectral(count, 2)),
        scratch(*spectral(count, 2)),
        scratch(*spectral(count, 4)),
    ]

    def call(kernel, name, outs, scratches, *args, in_specs=None, out_specs=None, cost=None):
        return pl.pallas_call(
            kernel,
            out_shape=outs,
            in_specs=in_specs or vmem(len(args)),
            out_specs=out_specs or vmem(len(outs)),
            scratch_shapes=scratches,
            compiler_params=params(),
            cost_estimate=cost
            and pl.CostEstimate(flops=cost, bytes_accessed=cost // 300, transcendentals=0),
            name=name,
        )(*args)

    winds = wind_field.reshape(2, lon_count, lat_count)
    far_first, far_second = from_antipode(winds), from_antipode(thickness)
    fields = jnp.concatenate([thickness, winds], 0)
    east, rest, near_pack, far_pack = call(
        gather_kernel, "gather_fields", [one, two, pack_shape, pack_shape], [], fields
    )
    height = thickness
    for step in range(STEPS):
        final = step == STEPS - 1
        counts = (2, 1) if step == 0 else (1, 2)
        near = exchange(near_pack, "lon", 0)
        levels = [exchange(height, "lev", first) for first in (0, 1)]
        far = exchange(far_pack, "lon", 1)
        spectra = call(
            functools.partial(own_kernel, blocks, counts[0]),
            "own_spectra",
            [array(*spectral(count, 2)) for count in counts],
            [scratch(*spectral(3, 2))],
            near,
            east,
            rest,
            twist,
            masks,
            *forward_tables,
            *inverse_tables,
            back,
            in_specs=anywhere(1) + vmem(9),
        )
        (zonal_terms,) = call(
            zonal_kernel,
            "zonal_terms",
            [array(3, lon_count, lat_count)],
            [],
            east,
            rest,
            near,
            far,
            rows,
            cost=LATE_ZONAL_COST if final else ZONAL_COST,
        )
        if final:
            break
        east_next, north_terms = call(
            functools.partial(first_kernel, blocks),
            "eastward_wind",
            [one, two],
            working(2),
            far_first,
            spectra[0],
            east,
            rest,
            zonal_terms,
            *tables,
            cost=FIRST_COST,
        )
        far_first = from_antipode(east_next)
        rest, height, near_pack, far_pack = call(
            functools.partial(second_kernel, blocks),
            "north_and_height",
            [two, one, pack_shape, pack_shape],
            working(1),
            far_second,
            spectra[1],
            rest,
            zonal_terms,
            north_terms,
            east_next,
            *levels,
            *tables,
            cost=SECOND_COST,
        )
        east = east_next
        far_second = from_antipode(rest)

    east_terms = call(
        functools.partial(transform_kernel, blocks, (-1,)),
        "transform_east",
        [one, one],
        working(1)[2:],
        far_first,
        spectra[0],
        *tables,
        cost=EAST_COST,
    )
    (fields,) = call(
        functools.partial(rest_kernel, blocks),
        "rest_fields",
        [array(3, lon_count, lat_count)],
        working(2),
        far_second,
        spectra[1],
        rest,
        zonal_terms,
        *east_terms,
        *tables,
        cost=REST_COST,
    )
    height, winds = call(
        last_kernel,
        "last_update",
        [one, two],
        [scratch(lon_count, lat_count), pltpu.SemaphoreType.DMA((3,))],
        fields,
        *levels,
        out_specs=anywhere(2),
    )
    return height, winds.reshape(wind_field.shape)


def solution(mesh):
    in_specs = (P("lev", "lon", None), P(None, "lev", "lon", None))
    out_specs = (P("lev", "lon", None), P(None, "lev", "lon", None))
    return jax.shard_map(body, mesh=mesh, in_specs=in_specs, out_specs=out_specs, check_vma=False)
```

```python
import functools
import math

import jax
import jax.numpy as jnp
import numpy as np
from jax import lax
from jax.experimental import pallas as pl
from jax.experimental.pallas import tpu as pltpu
from jax.sharding import PartitionSpec as P

STEPS = 2

courant = 0.2
mixing = 0.25
coriolis = 0.5
cos_floor = 0.25

RADIX = 128
ROWS = 8
FIRST_COST = 2_000_000_000
SECOND_COST = 2_000_000_000
EAST_COST = 1_500_000_000
REST_COST = 2_500_000_000
ZONAL_COST = 2000000000
LATE_ZONAL_COST = 1
PIECES = 4
HALO = 3


def split_table(table):
    high = table.astype(np.float32).astype(jnp.bfloat16)
    low = (table - high.astype(np.float64)).astype(np.float32).astype(jnp.bfloat16)
    return jnp.asarray(high), jnp.asarray(low)


@functools.lru_cache(maxsize=None)
def numpy_tables(lat_count):
    length = 2 * lat_count
    blocks = length // RADIX
    kept = blocks // 2 + 1
    centred = np.arange(RADIX) + 0.5
    order = np.arange(RADIX)
    signed = np.where(order < RADIX // 2, order, order - RADIX).astype(np.float64)
    angle = 2.0 * np.pi / RADIX * centred[:, None] * signed[None, :]
    cos, sin = np.cos(angle), np.sin(angle)
    forward = np.block([[cos, -sin], [sin, cos]])
    cos_t, sin_t = cos.T, sin.T
    weight = signed[:, None]
    inverse = np.block(
        [
            [cos_t, sin_t, -weight * sin_t, weight * cos_t],
            [-sin_t, cos_t, -weight * cos_t, -weight * sin_t],
        ]
    )
    first = np.arange(kept)
    turn = 2.0 * np.pi / length * first[:, None] * centred[None, :]
    twist = np.stack([np.cos(turn), -np.sin(turn)], 1)
    share = np.where((first == 0) | (first == blocks // 2), 1.0, 2.0)[:, None] / length
    back = np.stack([np.cos(turn) * share, np.sin(turn) * share], 1)
    slope_scale = 2.0 * np.pi * blocks / length
    back = np.concatenate([back, back * slope_scale], 1)
    wave = first[:, None] + blocks * signed[None, :]
    retained = (np.abs(wave) <= length // 3).astype(np.float64)
    plus = np.concatenate([retained, retained], 1)
    minus = np.concatenate([retained, -retained], 1)
    masks = np.stack([plus, minus, -minus], 1)
    latitude = (np.arange(lat_count) + 0.5) * (np.pi / lat_count) - 0.5 * np.pi
    rows = np.stack(
        [1.0 / np.maximum(np.cos(latitude), cos_floor), coriolis * np.sin(latitude)]
    )
    flat = lambda a: a.reshape(-1, a.shape[-1]).astype(np.float32)
    return forward, inverse, flat(twist), flat(back), flat(masks), rows.astype(np.float32)


def times(value, angle):
    real, imag = value
    cos, sin = math.cos(angle), math.sin(angle)
    quarter = round(angle / (math.pi / 2), 9)
    if quarter == int(quarter):
        turn = int(quarter) % 4
        return [(real, imag), (-imag, real), (-real, -imag), (imag, -real)][turn]
    if abs(abs(cos) - abs(sin)) < 1e-12:
        scale = abs(cos)
        a = real if cos > 0 else -real
        b = imag if cos > 0 else -imag
        c = imag if sin > 0 else -imag
        d = real if sin > 0 else -real
        return (scale * (a - c), scale * (b + d))
    return (real * cos - imag * sin, imag * cos + real * sin)


def add(a, b):
    return (a[0] + b[0], a[1] + b[1])


def sub(a, b):
    return (a[0] - b[0], a[1] - b[1])


def complex_dft(values, sign):
    n = len(values)
    if n == 1:
        return values
    half = n // 2
    even = complex_dft([add(values[m], values[m + half]) for m in range(half)], sign)
    odd = complex_dft(
        [
            times(sub(values[m], values[m + half]), sign * 2 * math.pi * m / n)
            for m in range(half)
        ],
        sign,
    )
    return [even[q // 2] if q % 2 == 0 else odd[q // 2] for q in range(n)]


def odd_outputs(values):
    r = len(values)
    if r == 1:
        return {1: (values[0], None)}
    half = r // 2
    turned = [
        times((values[m], -values[m + half]), -math.pi * m / r) for m in range(half)
    ]
    out = {}
    for q, value in enumerate(complex_dft(turned, -1)):
        j = 4 * q + 1
        out[j if j <= r else 2 * r - j] = value if j <= r else (value[0], -value[1])
    return out


def half_circle_forward(values):
    n = len(values)
    out = {j: value for j, value in odd_outputs(values).items()}
    scale = 2
    while len(values) > 1:
        half = len(values) // 2
        difference = [values[m] - values[m + half] for m in range(half)]
        values = [values[m] + values[m + half] for m in range(half)]
        for j, value in odd_outputs(difference).items():
            out[j * scale] = value
        scale *= 2
    out[0] = (values[0], None)
    return [out[k] for k in range(n + 1)]


def odd_inputs(values, r):
    if r == 1:
        return [values[1][0]]
    half = r // 2
    gathered = []
    for q in range(half):
        j = 4 * q + 1
        if j <= r:
            gathered.append(values[j])
        else:
            real, imag = values[2 * r - j]
            gathered.append((real, -imag))
    turned = [
        times(value, math.pi * m / r) for m, value in enumerate(complex_dft(gathered, 1))
    ]
    return [value[0] for value in turned] + [-value[1] for value in turned]


def half_circle_inverse(values):
    n = len(values) - 1
    result = [values[0][0]]
    size = 1
    while size < n:
        step = n // size
        difference = odd_inputs({j: values[j * step] for j in range(1, size + 1, 2)}, size)
        result = [result[m] + difference[m] for m in range(size)] + [
            result[m] - difference[m] for m in range(size)
        ]
        size *= 2
    last = odd_inputs({j: values[j] for j in range(1, n + 1, 2)}, n)
    return [result[m] + last[m] for m in range(n)]


def tile(index):
    return pl.ds(index * RADIX, RADIX)


def split(value):
    high = value.astype(jnp.bfloat16)
    return high, (value - high.astype(jnp.float32)).astype(jnp.bfloat16)


def triple_product(value, high_table, low_table):
    high, low = split(value)
    left = jnp.concatenate([high, low, high], 1)
    right = jnp.concatenate([high_table, high_table, low_table], 0)
    return jnp.dot(left, right, preferred_element_type=jnp.float32)


def forward_stage(slabs_of, groups, twist, turned, blocks):
    for group in range(groups):
        slabs = slabs_of(group)
        for k, (real, imag) in enumerate(half_circle_forward(slabs)):
            at = pl.ds((k * groups + group) * ROWS, ROWS)
            cos, sin = twist[2 * k : 2 * k + 1, :], twist[2 * k + 1 : 2 * k + 2, :]
            if imag is None:
                turned[at, tile(0)] = real * cos
                turned[at, tile(1)] = real * sin
            else:
                turned[at, tile(0)] = real * cos - imag * sin
                turned[at, tile(1)] = real * sin + imag * cos


def row_groups(lon_count):
    return [slice(i, i + ROWS) for i in range(0, lon_count, ROWS)]


def pack_rows(pack, lat_count, field, index, rows):
    if field < 2:
        pack[HALO * field : HALO * field + HALO, tile(index)] = rows
    else:
        pack[2 * HALO : ROWS, tile(index)] = rows[: ROWS - 2 * HALO]
        pack[index // 2 : index // 2 + 1, pl.ds(lat_count + index % 2 * RADIX, RADIX)] = rows[
            ROWS - 2 * HALO :
        ]


def halo_rows(pack, lat_count, field, index):
    if field < 2:
        return pack[HALO * field : HALO * field + HALO, tile(index)]
    last = pack[index // 2 : index // 2 + 1, pl.ds(lat_count + index % 2 * RADIX, RADIX)]
    return jnp.concatenate([pack[2 * HALO : ROWS, tile(index)], last], 0)


def field_at(east, rest, field, *at):
    return east[(0, *at)] if field == 0 else rest[(field - 1, *at)]


def odd_device():
    return lax.rem(lax.axis_index("lon"), 2) == 1


def pack_tile(field, index, rows, near_pack, far_pack, lat_count):
    first, last = rows[:HALO], rows[rows.shape[0] - HALO :]
    odd = odd_device()
    pack_rows(near_pack, lat_count, field, index, jnp.where(odd, first, last))
    pack_rows(far_pack, lat_count, field, index, jnp.where(odd, last, first))


def gather_kernel(fields, east, rest, near_pack, far_pack):
    lat_count = fields.shape[-1]
    for index in range(lat_count // RADIX):
        at = tile(index)
        thickness, eastward, northward = [fields[i, :, at] for i in range(3)]
        east[0, :, at] = eastward
        rest[0, :, at] = northward
        rest[1, :, at] = thickness
        for field, rows in enumerate((eastward, northward, thickness)):
            pack_tile(field, index, rows, near_pack, far_pack, lat_count)


def own_kernel(blocks, split_at, near, east, rest, twist, masks, high, low, *refs):
    first, second, turned = refs[-3:]
    kept = blocks // 2 + 1
    lon_count = east.shape[1]
    groups = [(field, at) for field in range(3) for at in row_groups(lon_count)]

    def slabs_of(group):
        field, at = groups[group]
        return [field_at(east, rest, field, at, tile(m)) for m in range(blocks // 2)]

    forward_stage(slabs_of, len(groups), twist, turned, blocks)
    result = triple_product(turned[...], high[...], low[...])
    cut, span = split_at * lon_count, 3 * lon_count
    for k in range(kept):
        value = result[k * span : k * span + span, :] * masks[3 * k : 3 * k + 1, :]
        first[k * cut : k * cut + cut, :] = value[:cut]
        second[k * (span - cut) : (k + 1) * (span - cut), :] = value[cut:]


def transform(blocks, parities, far, spectrum, tables, smooth, slope, work):
    twist, back, masks, forward_high, forward_low, inverse_high, inverse_low = tables
    turned, weighted, spread = work
    kept = blocks // 2 + 1
    count, lon_count = far.shape[:2]
    length = blocks * RADIX
    groups = [(field, at) for field in range(count) for at in row_groups(lon_count)]

    def slabs_of(group):
        field, at = groups[group]
        return [far[field, at, tile(m)] for m in range(blocks // 2)]

    forward_stage(slabs_of, len(groups), twist, turned, blocks)
    result = triple_product(turned[...], forward_high[...], forward_low[...])
    for k in range(kept):
        for field, parity in enumerate(parities):
            at = (k * count + field) * lon_count
            row = 3 * k + (1 if parity > 0 else 2)
            weighted[at : at + lon_count, :] = (
                spectrum[at : at + lon_count, :]
                + result[at : at + lon_count, :] * masks[row : row + 1, :]
            )
    spread[...] = triple_product(weighted[...], inverse_high[...], inverse_low[...])
    for group, (field, out) in enumerate(groups):
        smooth_terms, slope_terms = [], []
        for k in range(kept):
            at = pl.ds((k * len(groups) + group) * ROWS, ROWS)
            real, imag, slope_real, slope_imag = [spread[at, tile(i)] for i in range(4)]
            cos, sin, slope_cos, slope_sin = [back[4 * k + i : 4 * k + i + 1, :] for i in range(4)]
            turn_real = real * cos - imag * sin
            turn_imag = real * sin + imag * cos
            wave = 2.0 * math.pi * k / length
            smooth_terms.append((turn_real, turn_imag))
            slope_terms.append(
                (
                    slope_real * slope_cos - slope_imag * slope_sin - wave * turn_imag,
                    slope_real * slope_sin + slope_imag * slope_cos + wave * turn_real,
                )
            )
        for m, value in enumerate(half_circle_inverse(smooth_terms)):
            smooth[field, out, tile(m)] = value
        for m, value in enumerate(half_circle_inverse(slope_terms)):
            slope[field, out, tile(m)] = value


def zonal_parts(index, east, rest, near, far, rows):
    lon_count, lat_count = east.shape[1:]
    odd = odd_device()
    here = [field_at(east, rest, field, slice(None), tile(index)) for field in range(3)]
    secant, turning = rows[0:1, tile(index)], rows[1:2, tile(index)]
    zonal = []
    for field in range(3):
        close = halo_rows(near, lat_count, field, index)
        away = halo_rows(far, lat_count, field, index)
        line = jnp.concatenate(
            [jnp.where(odd, close, away), here[field], jnp.where(odd, away, close)], 0
        )
        at = [line[i : i + lon_count] for i in range(2 * HALO + 1)]
        difference = (
            (45.0 / 60.0) * (at[4] - at[2])
            - (9.0 / 60.0) * (at[5] - at[1])
            + (1.0 / 60.0) * (at[6] - at[0])
        )
        zonal.append(secant * difference)
    eastward, northward, thick = here
    return here, (
        turning * northward - eastward * zonal[0] - zonal[2],
        -eastward * zonal[1] - turning * eastward,
        -eastward * zonal[2] - thick * zonal[0],
    )


def first_kernel(blocks, far_rows, spectrum, east, rest, zonal_terms, *refs):
    tables, refs = refs[:7], refs[7:]
    east_next, north_terms, smooth, slope, *work = refs
    transform(blocks, (-1, -1), far_rows, spectrum, tables, smooth, slope, work)
    north_terms[0] = smooth[1]
    north_terms[1] = slope[1]
    for index in range(east.shape[-1] // RADIX):
        at = tile(index)
        tendency = zonal_terms[0, :, at] - rest[0, :, at] * slope[0, :, at]
        east_next[0, :, at] = smooth[0, :, at] + courant * tendency


def second_kernel(
    blocks, far_rows, spectrum, rest, zonal_terms, north_terms, east_next, levels, others, *refs
):
    tables, refs = refs[:7], refs[7:]
    rest_next, height_next, near_pack, far_pack, smooth, slope, *work = refs
    lat_count = rest.shape[-1]
    transform(blocks, (1,), far_rows, spectrum, tables, smooth, slope, work)
    for index in range(lat_count // RADIX):
        at = tile(index)
        northward, thick = rest[0, :, at], rest[1, :, at]
        north_slope, thick_slope = north_terms[1, :, at], slope[0, :, at]
        vertical = levels[0, :, at] + others[0, :, at] - 2.0 * thick
        north_tendency = zonal_terms[1, :, at] - northward * north_slope - thick_slope
        thick_tendency = (
            zonal_terms[2, :, at]
            - northward * thick_slope
            - thick * north_slope
            + mixing * vertical
        )
        values = (
            north_terms[0, :, at] + courant * north_tendency,
            smooth[0, :, at] + courant * thick_tendency,
        )
        for field in range(2):
            rest_next[field, :, at] = values[field]
        height_next[0, :, at] = values[1]
        for field, moved in enumerate((east_next[0, :, at], *values)):
            pack_tile(field, index, moved, near_pack, far_pack, lat_count)


def transform_kernel(blocks, parities, far_rows, spectrum, *refs):
    tables, (smooth, slope, *work) = refs[:7], refs[7:]
    transform(blocks, parities, far_rows, spectrum, tables, smooth, slope, work)


def zonal_kernel(east, rest, near, far, rows, out):
    for index in range(east.shape[-1] // RADIX):
        _, terms = zonal_parts(index, east, rest, near, far, rows)
        for field in range(3):
            out[field, :, tile(index)] = terms[field]


def rest_kernel(
    blocks, far_rows, spectrum, rest, zonal_terms, east_smooth, east_slope, *refs
):
    tables, (out, smooth, slope, *work) = refs[:7], refs[7:]
    transform(blocks, (-1, 1), far_rows, spectrum, tables, smooth, slope, work)
    for index in range(rest.shape[-1] // RADIX):
        at = tile(index)
        northward, thick = rest[0, :, at], rest[1, :, at]
        north_slope, thick_slope = slope[0, :, at], slope[1, :, at]
        tendencies = (
            zonal_terms[0, :, at] - northward * east_slope[0, :, at],
            zonal_terms[1, :, at] - northward * north_slope - thick_slope,
            zonal_terms[2, :, at]
            - northward * thick_slope
            - thick * north_slope
            - 2.0 * mixing * thick,
        )
        smooths = (east_smooth[0, :, at], smooth[0, :, at], smooth[1, :, at])
        for field in range(3):
            out[field, :, at] = smooths[field] + courant * tendencies[field]


def last_kernel(fields, levels, others, height_out, wind_out, height, sems):
    copies = [
        pltpu.make_async_copy(fields.at[0], wind_out.at[0], sems.at[0]),
        pltpu.make_async_copy(fields.at[1], wind_out.at[1], sems.at[1]),
        pltpu.make_async_copy(height, height_out.at[0], sems.at[2]),
    ]
    copies[0].start()
    copies[1].start()
    for index in range(height.shape[-1] // RADIX):
        at = tile(index)
        neighbours = levels[0, :, at] + others[0, :, at]
        height[:, at] = fields[2, :, at] + (courant * mixing) * neighbours
    copies[2].start()
    for copy in copies:
        copy.wait()


def vmem(count):
    return [pl.BlockSpec(memory_space=pltpu.VMEM)] * count


def anywhere(count):
    return [pl.BlockSpec(memory_space=pl.ANY)] * count


def params():
    return pltpu.CompilerParams(vmem_limit_bytes=24 * 1024 * 1024)


def exchange(value, axis, first):
    size = lax.axis_size(axis)
    wrap = axis == "lon"
    pairs = [(i, (i + 1) % size) for i in range(first, size if wrap else size - 1, 2)]
    return lax.ppermute(value, axis, pairs + [(j, i) for i, j in pairs])


def from_antipode(value):
    size = lax.axis_size("lon")
    return lax.ppermute(value, "lon", [(i, (i + size // 2) % size) for i in range(size)])


def body(thickness, wind_field):
    level_count, lon_count, lat_count = thickness.shape
    assert level_count == 1 and lon_count % ROWS == 0
    blocks = 2 * lat_count // RADIX
    kept = blocks // 2 + 1
    forward, inverse, twist, back, masks, rows = numpy_tables(lat_count)
    forward_tables = split_table(forward)
    inverse_tables = split_table(inverse)
    twist, back, masks, rows = [jnp.asarray(a) for a in (twist, back, masks, rows)]
    tables = (twist, back, masks, *forward_tables, *inverse_tables)
    f32 = jnp.float32
    array = lambda *shape: jax.ShapeDtypeStruct(shape, f32)
    scratch = lambda *shape: pltpu.VMEM(shape, f32)
    one, two = array(1, lon_count, lat_count), array(2, lon_count, lat_count)
    pack_shape = array(ROWS, lat_count + lat_count // ROWS)
    spectral = lambda count, width: (count * kept * lon_count, width * RADIX)
    working = lambda count: [
        scratch(count, lon_count, lat_count),
        scratch(count, lon_count, lat_count),
        scratch(*spectral(count, 2)),
        scratch(*spectral(count, 2)),
        scratch(*spectral(count, 4)),
    ]

    def call(kernel, name, outs, scratches, *args, in_specs=None, out_specs=None, cost=None):
        return pl.pallas_call(
            kernel,
            out_shape=outs,
            in_specs=in_specs or vmem(len(args)),
            out_specs=out_specs or vmem(len(outs)),
            scratch_shapes=scratches,
            compiler_params=params(),
            cost_estimate=cost
            and pl.CostEstimate(flops=cost, bytes_accessed=cost // 300, transcendentals=0),
            name=name,
        )(*args)

    winds = wind_field.reshape(2, lon_count, lat_count)
    far_first, far_second = from_antipode(winds), from_antipode(thickness)
    fields = jnp.concatenate([thickness, winds], 0)
    east, rest, near_pack, far_pack = call(
        gather_kernel, "gather_fields", [one, two, pack_shape, pack_shape], [], fields
    )
    height = thickness
    for step in range(STEPS):
        final = step == STEPS - 1
        counts = (2, 1) if step == 0 else (1, 2)
        near = exchange(near_pack, "lon", 0)
        levels = [exchange(height, "lev", first) for first in (0, 1)]
        far = exchange(far_pack, "lon", 1)
        spectra = call(
            functools.partial(own_kernel, blocks, counts[0]),
            "own_spectra",
            [array(*spectral(count, 2)) for count in counts],
            [scratch(*spectral(3, 2))],
            near,
            east,
            rest,
            twist,
            masks,
            *forward_tables,
            *inverse_tables,
            back,
            in_specs=anywhere(1) + vmem(9),
        )
        (zonal_terms,) = call(
            zonal_kernel,
            "zonal_terms",
            [array(3, lon_count, lat_count)],
            [],
            east,
            rest,
            near,
            far,
            rows,
            cost=LATE_ZONAL_COST if final else ZONAL_COST,
        )
        if final:
            break
        east_next, north_terms = call(
            functools.partial(first_kernel, blocks),
            "eastward_wind",
            [one, two],
            working(2),
            far_first,
            spectra[0],
            east,
            rest,
            zonal_terms,
            *tables,
            cost=FIRST_COST,
        )
        far_first = from_antipode(east_next)
        rest, height, near_pack, far_pack = call(
            functools.partial(second_kernel, blocks),
            "north_and_height",
            [two, one, pack_shape, pack_shape],
            working(1),
            far_second,
            spectra[1],
            rest,
            zonal_terms,
            north_terms,
            east_next,
            *levels,
            *tables,
            cost=SECOND_COST,
        )
        east = east_next
        far_second = from_antipode(rest)

    east_terms = call(
        functools.partial(transform_kernel, blocks, (-1,)),
        "transform_east",
        [one, one],
        working(1)[2:],
        far_first,
        spectra[0],
        *tables,
        cost=EAST_COST,
    )
    (fields,) = call(
        functools.partial(rest_kernel, blocks),
        "rest_fields",
        [array(3, lon_count, lat_count)],
        working(2),
        far_second,
        spectra[1],
        rest,
        zonal_terms,
        *east_terms,
        *tables,
        cost=REST_COST,
    )
    height, winds = call(
        last_kernel,
        "last_update",
        [one, two],
        [scratch(lon_count, lat_count), pltpu.SemaphoreType.DMA((3,))],
        fields,
        *levels,
        out_specs=anywhere(2),
    )
    return height, winds.reshape(wind_field.shape)


def solution(mesh):
    in_specs = (P("lev", "lon", None), P(None, "lev", "lon", None))
    out_specs = (P("lev", "lon", None), P(None, "lev", "lon", None))
    return jax.shard_map(body, mesh=mesh, in_specs=in_specs, out_specs=out_specs, check_vma=False)
```
